512 devices in a mesh: lat: 32 (over x_hi, z, core), lon: 16 (over x_lo, y).
Axes of the slice: x: 4 (x_hi: 2, x_lo: 2; x = x_hi * 2 + x_lo), y: 8, z: 8, core: 2. Of those that a mesh axis runs over, the one named last changes fastest.
Arguments:
- winds: float32 [2, 288, 46080], P(None, 'lat', 'lon'), as said below
- thickness: float32 [288, 46080], P('lat', 'lon'), may hold values from 0.5 to 1.5
- tracers: bfloat16 [3, 288, 46080], P(None, 'lat', 'lon'), may hold values from 0 to 1
- cutoff: int32 [288], replicated, may hold values from 1 to 1440, as said below
Outputs:
- new_winds: float32 [2, 288, 46080], P(None, 'lat', 'lon')
- new_thickness: float32 [288, 46080], P('lat', 'lon')
- tracer_mass: bfloat16 [3, 288, 46080], P(None, 'lat', 'lon')
The draws below stay inside these ranges and needn't reach their ends.
Inputs may be any that keep to these rules, and one draw needn't show every extreme that they name: `cutoff`: the 48 rows nearest each pole have cutoffs that grow from 1 at the pole row to at most a quarter of 2880; every other row has exactly 1440, so that the filter leaves it unchanged. `winds`: each wind is the cosine of its row's latitude times a value of order one.
All inputs are finite; a program needn't handle non-finite values.
Results may differ from the reference program's by a relative error of at most 0.001.
Values sent between devices are 32-bit elements; how exact they have to be, the bound alone decides.
A program may use at most 64 MiB of HBM per device.

```python
import math
import jax
import jax.numpy as jnp
from jax import lax

LEVELS = 16
NLAT = 288
NLON = 2880
POLAR = 48


def draw_winds(key, part):
    rows = jnp.arange(NLAT, dtype=jnp.float32)
    centre = (rows + 0.5) * (math.pi / NLAT) - math.pi / 2
    scale = jnp.cos(centre)[None, :, None]
    shape = (2, NLAT, NLON * LEVELS)
    values = jax.random.normal(key, shape, jnp.float32)
    return (values * scale).astype(jnp.float32)


def draw_cutoff(key, part):
    index = jnp.arange(NLAT, dtype=jnp.int32)
    distance = jnp.minimum(index, NLAT - 1 - index)
    jitter = jax.random.randint(key, (NLAT,), 0, 3, dtype=jnp.int32)
    polar_value = 1 + distance * (NLON // 4 - 3) // POLAR + jnp.where(distance > 0, jitter, 0)
    return jnp.where(distance < POLAR, polar_value, NLON // 2).astype(jnp.int32)


def levels(key, dims, shards, low, top_value):
    def one(axis_at, shards_of):
        steps = jax.random.uniform(jax.random.fold_in(jax.random.fold_in(key, 6), axis_at), (shards_of,), jnp.float32, low / len(shards), top_value / len(shards))
        return jnp.repeat(jnp.exp(steps), dims[axis_at] // shards_of).reshape((-1,) + (1,) * (len(dims) - axis_at - 1))

    gain = one(*shards[0])
    for cut in shards[1:]:
        gain = gain * one(*cut)
    return gain


def setup_inputs(seed: int = 0) -> dict:
    seeds = jax.random.split(jax.random.key(seed), 5)
    winds = draw_winds(jax.random.fold_in(seeds[4], 71), 0)
    thickness = jnp.clip(0.5 + 1.0 * jax.random.uniform(seeds[1], (NLAT, NLON * LEVELS), jnp.float32) ** levels(seeds[1], (NLAT, NLON * LEVELS), ((0, 32), (1, 16)), -0.2, 0.2), 0.5, 1.5)
    tracers = jnp.clip(1.0 * jax.random.uniform(seeds[2], (3, NLAT, NLON * LEVELS), jnp.float32) ** levels(seeds[2], (3, NLAT, NLON * LEVELS), ((1, 32), (2, 16)), -0.2, 0.2), 0.0, 1.0).astype(jnp.bfloat16)
    cutoff = draw_cutoff(jax.random.fold_in(seeds[4], 71), 0)
    return {"winds": winds, "thickness": thickness, "tracers": tracers, "cutoff": cutoff}


TIME_STEP = 0.05
DIFFUSION = 0.5


def grid_rows(first_row, count, nlat):
    index = first_row + jnp.arange(count, dtype=jnp.int32)
    centre = (index.astype(jnp.float32) + 0.5) * (math.pi / nlat) - math.pi / 2

    def face(row_index):
        inside = (row_index >= 0) & (row_index < nlat - 1)
        return jnp.where(inside, jnp.sin((row_index + 1).astype(jnp.float32) * (math.pi / nlat)), 0.0)

    return (jnp.cos(centre)[:, None], jnp.sin(centre)[:, None], face(index)[:, None], face(index - 1)[:, None])


def tendencies(thick, wind_u, wind_v, tracer, thick_e, thick_w, wind_ue, wind_uw, tracer_e, tracer_w,
               thick_n, thick_s, wind_vn, wind_vs, tracer_n, tracer_s, cos_centre, sin_centre, cos_north,
               cos_south, ratio):
    flux_east = 0.5 * (wind_u + wind_ue) * (0.5 * (thick + thick_e))
    flux_west = 0.5 * (wind_uw + wind_u) * (0.5 * (thick_w + thick))
    flux_north = 0.5 * (wind_v + wind_vn) * (0.5 * (thick + thick_n)) * cos_north
    flux_south = 0.5 * (wind_vs + wind_v) * (0.5 * (thick_s + thick)) * cos_south
    thick_tend = -((flux_east - flux_west) + ratio * (flux_north - flux_south)) / cos_centre
    wind_u_tend = sin_centre * wind_v - (thick_e - thick_w) / (2.0 * cos_centre)
    wind_v_tend = -sin_centre * wind_u - ratio * (thick_n - thick_s) * 0.5
    zonal_part = flux_east * (0.5 * (tracer + tracer_e)) - flux_west * (0.5 * (tracer_w + tracer))
    merid_part = flux_north * (0.5 * (tracer + tracer_n)) - flux_south * (0.5 * (tracer_s + tracer))
    tracer_flux = (zonal_part + ratio * merid_part) / cos_centre
    laplace = (tracer_e + tracer_w) + (tracer_n + tracer_s) - 4.0 * tracer
    tracer_mass = thick * tracer + TIME_STEP * (DIFFUSION * laplace - tracer_flux)
    return thick_tend, wind_u_tend, wind_v_tend, tracer_mass


def zonal_filter(field, cutoff, nlon):
    spectrum = jnp.fft.rfft(field, axis=-1)
    wave = jnp.arange(nlon // 2 + 1, dtype=jnp.int32)
    keep = wave[None, :] <= cutoff[:, None]
    return jnp.fft.irfft(jnp.where(keep, spectrum, 0.0), n=nlon, axis=-1).astype(jnp.float32)


def reference(winds, thickness, tracers, cutoff):
    nlat = thickness.shape[0]
    nlon = thickness.shape[1] // LEVELS
    half = nlon // 2
    ratio = 2.0 * nlat / nlon
    cos_centre, sin_centre, cos_north, cos_south = grid_rows(0, nlat, nlat)

    def unpack(field):
        shaped = field.reshape(field.shape[:-2] + (nlat, nlon, LEVELS))
        return jnp.moveaxis(shaped, -1, -3)

    def pack(field):
        moved = jnp.moveaxis(field, -3, -1)
        return moved.reshape(moved.shape[:-3] + (nlat, nlon * LEVELS))

    def east(field):
        return jnp.roll(field, -1, axis=-1)

    def west(field):
        return jnp.roll(field, 1, axis=-1)

    def north(field, sign):
        return jnp.concatenate([field[..., 1:, :], sign * jnp.roll(field[..., -1:, :], half, axis=-1)], axis=-2)

    def south(field, sign):
        return jnp.concatenate([sign * jnp.roll(field[..., :1, :], half, axis=-1), field[..., :-1, :]], axis=-2)

    def one_level(inputs):
        thick, wind_u, wind_v, tracer = inputs
        thick_tend, wind_u_tend, wind_v_tend, tracer_mass = tendencies(
            thick, wind_u, wind_v, tracer, east(thick), west(thick), east(wind_u), west(wind_u),
            east(tracer), west(tracer), north(thick, 1.0), south(thick, 1.0), north(wind_v, -1.0),
            south(wind_v, -1.0), north(tracer, 1.0), south(tracer, 1.0), cos_centre, sin_centre,
            cos_north, cos_south, ratio)
        new_thick = thick + TIME_STEP * zonal_filter(thick_tend, cutoff, nlon)
        new_u = wind_u + TIME_STEP * zonal_filter(wind_u_tend, cutoff, nlon)
        new_v = wind_v + TIME_STEP * zonal_filter(wind_v_tend, cutoff, nlon)
        return new_thick, new_u, new_v, tracer_mass

    level_winds = unpack(winds)
    level_tracers = unpack(tracers.astype(jnp.float32))
    new_thick, new_u, new_v, masses = lax.map(
        one_level, (unpack(thickness), level_winds[0], level_winds[1], jnp.moveaxis(level_tracers, 1, 0)))
    mass_out = pack(jnp.moveaxis(masses, 0, 1)).astype(jnp.bfloat16)
    return pack(jnp.stack([new_u, new_v])), pack(new_thick), mass_out
```

```python
import functools
import math

import jax
import jax.numpy as jnp
import numpy as np
from jax import lax
from jax.experimental import pallas as pl
from jax.experimental.pallas import tpu as pltpu
from jax.sharding import PartitionSpec as P

MESH = pl.DeviceIdType.MESH
F32 = jnp.float32
BF16 = jnp.bfloat16

LEVELS = 16
NLAT = 288
NLON = 2880
POLAR = 48
TIME_STEP = 0.05
DIFFUSION = 0.5
RATIO = 2.0 * NLAT / NLON

N_LAT = 32
N_LON = 16
ROWS = NLAT // N_LAT
COLS = NLON // N_LON
WIDE = COLS * LEVELS

LANES = 128
PER = LANES // LEVELS
TILES = 24
FULL = WIDE // LANES
TAIL = WIDE - FULL * LANES
FIELDS = 6
SLOT = FIELDS * TILES
EDGE = 5 * TILES
PAIRS = 3 * ROWS
BLOCK = TILES
OWN = N_LON
AWAY = PAIRS - OWN

BASE = NLON // PER
HALF = BASE // 2 + 1
FREQ = 184
SIDE = N_LON // 2 * TILES


def geometry():
    row = np.arange(NLAT, dtype=np.float64)
    centre = (row + 0.5) * (math.pi / NLAT) - math.pi / 2

    def face(index):
        inside = (index >= 0) & (index < NLAT - 1)
        return np.where(inside, np.sin((index + 1) * (math.pi / NLAT)), 0.0)

    table = np.stack([1.0 / np.cos(centre), np.sin(centre), face(row), face(row - 1)], axis=1)
    return table.astype(np.float32).reshape(-1)


def split_table(table):
    high = table.astype(np.float32).astype(jnp.bfloat16)
    low = (table - high.astype(np.float64)).astype(np.float32).astype(jnp.bfloat16)
    return np.concatenate([high, low], axis=0)


def filter_tables():
    turn = 2.0 * math.pi
    freq = np.arange(FREQ)
    live = (freq < HALF).astype(np.float64)
    sector, tile = (a.reshape(-1) for a in np.meshgrid(np.arange(N_LON // 2), np.arange(TILES), indexing="ij"))
    used = (tile * PER < COLS).astype(np.float64)
    place = 2 * COLS * sector // PER + tile
    angle = turn * ((freq[:, None] * place[None, :]) % BASE) / BASE
    weight = live[:, None] * used[None, :]
    fore = np.concatenate([np.cos(angle) * weight, -np.sin(angle) * weight], axis=0)
    twice = np.where((freq == 0) | (freq == HALF - 1), 1.0, 2.0) / NLON
    back = np.concatenate([np.cos(angle) * weight * twice[:, None], -np.sin(angle) * weight * twice[:, None]], axis=0).T

    lane = np.arange(2 * LANES)
    shift = lane % LANES // LEVELS + COLS * (lane // LANES)
    angle = turn * ((freq[:, None] * shift[None, :]) % NLON) / NLON
    twiddle = np.concatenate([np.cos(angle), np.sin(angle)], axis=0).astype(np.float32)

    out = np.arange(LANES)
    angle = turn * ((BASE * shift[:, None] * (out // LEVELS)[None, :]) % NLON) / NLON
    same = (lane % LEVELS)[:, None] == (out % LEVELS)[None, :]
    cosine, sine = np.cos(angle) * same, np.sin(angle) * same
    mix = np.concatenate(
        [np.concatenate([cosine, -sine], axis=1), np.concatenate([sine, cosine], axis=1)], axis=0
    )
    return split_table(fore), twiddle, split_table(mix), split_table(mix.T), split_table(back)


def split(value):
    high = value.astype(BF16)
    low = (value - high.astype(F32)).astype(BF16)
    return high, low


def dot(a, b):
    return jnp.dot(a, b, preferred_element_type=F32)


def table_left(table, rows, value):
    high, low = split(value)
    first = table[pl.ds(0, rows), :]
    return dot(first, high) + dot(first, low) + dot(table[pl.ds(rows, rows), :], high)


def table_right(value, table, rows):
    high, low = split(value)
    first = table[pl.ds(0, rows), :]
    return dot(high, first) + dot(low, first) + dot(high, table[pl.ds(rows, rows), :])


def eastward(value):
    lane = lax.broadcasted_iota(jnp.int32, (TILES, LANES), 1)
    here = pltpu.roll(value, LANES - LEVELS, 1)
    return jnp.where(lane < LANES - LEVELS, here, pltpu.roll(here, TILES - 1, 0))


def westward(value):
    lane = lax.broadcasted_iota(jnp.int32, (TILES, LANES), 1)
    here = pltpu.roll(value, LEVELS, 1)
    return jnp.where(lane >= LEVELS, here, pltpu.roll(here, 1, 0))


def kernel(
    cut, geo, winds_in, thick_in, mass_in, fore_in, twiddle_in, mix_in, unmix_in, back_in,
    winds_out, thick_out, mass_out,
    wv, hv, qv, mv, cells, to_east, to_west, from_west, from_east, tend, gathered, sent_back, returned, mass,
    fore, twiddle, mix, unmix, back,
    in_sem, table_sem, out_sem, halo_send, halo_recv, go_send, go_recv, back_send, back_recv,
):
    lat = lax.axis_index("lat")
    lon = lax.axis_index("lon")
    polar_south = lat * ROWS < POLAR
    polar_north = (lat + 1) * ROWS > NLAT - POLAR
    polar = jnp.logical_or(polar_south, polar_north)
    other = (lat + N_LAT // 2) % N_LAT
    other_polar = jnp.logical_or(other * ROWS < POLAR, (other + 1) * ROWS > NLAT - POLAR)
    lends = jnp.logical_and(other_polar, lon < AWAY)

    loads = [
        pltpu.make_async_copy(winds_in, wv, in_sem.at[0]),
        pltpu.make_async_copy(thick_in, hv, in_sem.at[1]),
        pltpu.make_async_copy(mass_in, qv, in_sem.at[2]),
    ]
    for load in loads:
        load.start()
    tables = [
        pltpu.make_async_copy(source, target, table_sem.at[i])
        for i, (source, target) in enumerate(
            ((fore_in, fore), (twiddle_in, twiddle), (mix_in, mix), (unmix_in, unmix), (back_in, back))
        )
    ]
    for load in tables:
        load.start()

    east = (lat, (lon + 1) % N_LON)
    west = (lat, (lon + N_LON - 1) % N_LON)
    below = (lat + N_LAT - 1) // N_LAT
    above = 1 - lat // (N_LAT - 1)
    south = (lat - below, (lon + (1 - below) * (N_LON // 2)) % N_LON)
    north = (lat + above, (lon + (1 - above) * (N_LON // 2)) % N_LON)

    barrier = pltpu.get_barrier_semaphore()

    def greet(device):
        pl.semaphore_signal(barrier, inc=1, device_id=device, device_id_type=MESH)

    for device in (east, west, south, north):
        greet(device)

    @pl.when(polar)
    def _():
        lax.fori_loop(1, N_LON, lambda i, c: (greet((lat, (lon + i) % N_LON)), c)[1], 0)
        lax.fori_loop(0, AWAY, lambda i, c: (greet((other, i)), c)[1], 0)

    @pl.when(lends)
    def _():
        lax.fori_loop(0, N_LON, lambda i, c: (greet((other, i)), c)[1], 0)

    for load in loads:
        load.wait()

    fields = (
        lambda at: hv[:, at],
        lambda at: wv[1, :, at],
        lambda at: qv[0, :, at].astype(F32),
        lambda at: qv[1, :, at].astype(F32),
        lambda at: qv[2, :, at].astype(F32),
        lambda at: wv[0, :, at],
    )

    def spread(t, carry):
        at = pl.ds(pl.multiple_of(t * LANES, LANES), LANES)
        for f, get in enumerate(fields):
            cells[pl.ds(SLOT + f * TILES + t, ROWS, stride=SLOT), :] = get(at)
        return carry

    lax.fori_loop(0, FULL, spread, 0)
    blank = jnp.zeros((ROWS, LANES - TAIL), F32)
    for f, get in enumerate(fields):
        last = jnp.concatenate([get(pl.ds(FULL * LANES, TAIL)), blank], axis=1)
        cells[pl.ds(SLOT + f * TILES + FULL, ROWS, stride=SLOT), :] = last

    sides = (0, 2, 3, 4, 5)
    for i, f in enumerate(sides):
        get = fields[f]
        to_west[pl.ds(i * ROWS, ROWS), :] = pltpu.roll(get(pl.ds(0, LANES)), TAIL, 1)
        last = jnp.concatenate([get(pl.ds(FULL * LANES, TAIL)), blank], axis=1)
        to_east[pl.ds(i * ROWS, ROWS), :] = pltpu.roll(last, LANES - TAIL, 1)

    @pl.when(polar)
    def _():
        pl.semaphore_wait(barrier, 4 + N_LON - 1 + AWAY)

    @pl.when(lends)
    def _():
        pl.semaphore_wait(barrier, 4 + N_LON)

    @pl.when(jnp.logical_not(jnp.logical_or(polar, lends)))
    def _():
        pl.semaphore_wait(barrier, 4)

    south_slot = below * (ROWS + 1)
    north_slot = (1 - above) * (ROWS + 1)

    def edge(slot):
        return cells.at[pl.ds(pl.multiple_of(slot * SLOT, 8), EDGE), :]

    halos = [
        pltpu.make_async_remote_copy(
            edge(1), edge(south_slot), halo_send.at[0], halo_recv.at[below], device_id=south, device_id_type=MESH
        ),
        pltpu.make_async_remote_copy(
            edge(ROWS), edge(north_slot), halo_send.at[1], halo_recv.at[1 - above],
            device_id=north, device_id_type=MESH,
        ),
        pltpu.make_async_remote_copy(
            to_east, from_west, halo_send.at[2], halo_recv.at[2], device_id=east, device_id_type=MESH
        ),
        pltpu.make_async_remote_copy(
            to_west, from_east, halo_send.at[3], halo_recv.at[3], device_id=west, device_id_type=MESH
        ),
    ]
    for halo in halos:
        halo.start()
    pltpu.make_async_copy(edge(0), edge(0), halo_recv.at[0]).wait()
    pltpu.make_async_copy(edge(ROWS + 1), edge(ROWS + 1), halo_recv.at[1]).wait()
    pltpu.make_async_copy(from_west, from_west, halo_recv.at[2]).wait()
    pltpu.make_async_copy(from_east, from_east, halo_recv.at[3]).wait()
    halos[0].wait_send()
    halos[1].wait_send()

    lane = lax.broadcasted_iota(jnp.int32, (ROWS, LANES), 1)
    for i, f in enumerate(sides):
        at = pl.ds(SLOT + f * TILES + FULL, ROWS, stride=SLOT)
        here = from_east[pl.ds(i * ROWS, ROWS), :]
        cells[at, :] = jnp.where((lane >= TAIL) & (lane < TAIL + LEVELS), here, cells[at, :])
        at = pl.ds(SLOT + f * TILES + FULL + 1, ROWS, stride=SLOT)
        here = from_west[pl.ds(i * ROWS, ROWS), :]
        cells[at, :] = jnp.where(lane >= LANES - LEVELS, here, 0.0)

    @pl.when(lat == 0)
    def _():
        cells[pl.ds(TILES, TILES), :] = -cells[pl.ds(TILES, TILES), :]

    @pl.when(lat == N_LAT - 1)
    def _():
        at = pl.ds((ROWS + 1) * SLOT + TILES, TILES)
        cells[at, :] = -cells[at, :]

    def row(slot, field):
        return cells[pl.ds(pl.multiple_of(slot * SLOT + field * TILES, 8), TILES), :]

    def scalars(j):
        at = (lat * ROWS + j) * 4
        return geo[at], geo[at + 1], geo[at + 2], geo[at + 3]

    flat = lax.broadcasted_iota(jnp.int32, (TILES, LANES), 0) * LANES + lax.broadcasted_iota(
        jnp.int32, (TILES, LANES), 1
    )
    valid = flat < WIDE

    def fluxes(j, cos_north, cos_south):
        h, h_n, h_s = row(j + 1, 0), row(j + 2, 0), row(j, 0)
        v, v_n, v_s = row(j + 1, 1), row(j + 2, 1), row(j, 1)
        u = row(j + 1, 5)
        h_e, h_w = eastward(h), westward(h)
        flux_e = 0.5 * (u + eastward(u)) * (0.5 * (h + h_e))
        flux_w = 0.5 * (westward(u) + u) * (0.5 * (h_w + h))
        flux_n = 0.5 * (v + v_n) * (0.5 * (h + h_n)) * cos_north
        flux_s = 0.5 * (v_s + v) * (0.5 * (h_s + h)) * cos_south
        return h, u, v, h_e, h_w, h_n, h_s, flux_e, flux_w, flux_n, flux_s

    def tendency(j, carry):
        inverse, sine, cos_north, cos_south = scalars(j)
        h, u, v, h_e, h_w, h_n, h_s, flux_e, flux_w, flux_n, flux_s = fluxes(j, cos_north, cos_south)
        values = (
            -((flux_e - flux_w) + RATIO * (flux_n - flux_s)) * inverse,
            sine * v - (h_e - h_w) * (0.5 * inverse),
            -sine * u - RATIO * (h_n - h_s) * 0.5,
        )
        for f, value in enumerate(values):
            at = pl.ds(pl.multiple_of((j * 3 + f) * BLOCK, 8), BLOCK)
            tend[at, :] = jnp.where(valid, value, 0.0)
        return carry

    lax.fori_loop(0, ROWS, tendency, 0)

    def block(ref, index):
        return ref.at[pl.ds(pl.multiple_of(index * BLOCK, 8), BLOCK), :]

    def place(sector):
        return (sector % 2) * (N_LON // 2) + sector // 2

    def go(pair, device):
        return pltpu.make_async_remote_copy(
            block(tend, pair), block(gathered, place(lon)), go_send, go_recv, device_id=device, device_id_type=MESH
        )

    @pl.when(polar)
    def _():
        def own(i, carry):
            target = (lon + i) % N_LON
            go(target, (lat, target)).start()
            return carry

        def away(i, carry):
            target = (lon + i) % AWAY
            go(OWN + target, (other, target)).start()
            return carry

        lax.fori_loop(0, AWAY, away, 0)
        lax.fori_loop(1, N_LON, own, 0)
        at = pl.ds(pl.multiple_of(place(lon) * BLOCK, 8), BLOCK)
        gathered[at, :] = tend[pl.ds(pl.multiple_of(lon * BLOCK, 8), BLOCK), :]

    def tracer(j, carry):
        inverse, sine, cos_north, cos_south = scalars(j)
        h, u, v, h_e, h_w, h_n, h_s, flux_e, flux_w, flux_n, flux_s = fluxes(j, cos_north, cos_south)
        for c in range(3):
            q, q_n, q_s = row(j + 1, 2 + c), row(j + 2, 2 + c), row(j, 2 + c)
            q_e, q_w = eastward(q), westward(q)
            zonal = flux_e * (0.5 * (q + q_e)) - flux_w * (0.5 * (q_w + q))
            merid = flux_n * (0.5 * (q + q_n)) - flux_s * (0.5 * (q_s + q))
            flux = (zonal + RATIO * merid) * inverse
            laplace = (q_e + q_w) + (q_n + q_s) - 4.0 * q
            at = pl.ds(pl.multiple_of((c * ROWS + j) * TILES, 8), TILES)
            mass[at, :] = h * q + TIME_STEP * (DIFFUSION * laplace - flux)
        return carry

    lax.fori_loop(0, ROWS, tracer, 0)

    def narrow(t, carry):
        at = pl.ds(pl.multiple_of(t * LANES, LANES), LANES)
        for c in range(3):
            mv[c, :, at] = mass[pl.ds(c * ROWS * TILES + t, ROWS, stride=TILES), :].astype(BF16)
        return carry

    lax.fori_loop(0, FULL, narrow, 0)
    for c in range(3):
        last = mass[pl.ds(c * ROWS * TILES + FULL, ROWS, stride=TILES), :]
        mv[c, :, pl.ds(FULL * LANES, TAIL)] = last[:, :TAIL].astype(BF16)
    stores = [pltpu.make_async_copy(mv, mass_out, out_sem.at[0])]
    stores[0].start()

    for load in tables:
        load.wait()

    def circle(pair_row):
        cutoff = cut[pair_row]
        data = jnp.concatenate([gathered[pl.ds(0, SIDE), :], gathered[pl.ds(SIDE, SIDE), :]], axis=1)
        lines = table_left(fore, 2 * FREQ, data)
        real, imag = lines[:FREQ], lines[FREQ:]
        cosine, sine = twiddle[pl.ds(0, FREQ), :], twiddle[pl.ds(FREQ, FREQ), :]
        turned = jnp.concatenate([real * cosine + imag * sine, imag * cosine - real * sine], axis=1)
        spectrum = table_right(turned, mix, 4 * LANES)
        wave = lax.broadcasted_iota(jnp.int32, (FREQ, 2 * LANES), 0) + BASE * (
            lax.broadcasted_iota(jnp.int32, (FREQ, 2 * LANES), 1) % LANES // LEVELS
        )
        wave = jnp.minimum(wave, NLON - wave)
        spectrum = jnp.where(wave <= cutoff, spectrum, 0.0)
        lines = table_right(spectrum, unmix, 2 * LANES)
        real, imag = lines[:, : 2 * LANES], lines[:, 2 * LANES :]
        turned = jnp.concatenate([real * cosine - imag * sine, real * sine + imag * cosine], axis=0)
        result = table_left(back, SIDE, turned)
        sent_back[pl.ds(0, SIDE), :] = result[:, :LANES]
        sent_back[pl.ds(SIDE, SIDE), :] = result[:, LANES:]

    def home(pair, sector, device):
        return pltpu.make_async_remote_copy(
            block(sent_back, place(sector)), block(returned, pair), back_send, back_recv,
            device_id=device, device_id_type=MESH,
        )

    def total(ref, blocks):
        return ref.at[pl.ds(0, blocks * BLOCK), :]

    def wait_for(ref, blocks, sem):
        pltpu.make_async_copy(total(ref, blocks), total(ref, blocks), sem).wait()

    @pl.when(polar)
    def _():
        wait_for(gathered, N_LON - 1, go_recv)
        circle(lat * ROWS + lon // 3)

        def own(i, carry):
            target = (lon + i) % N_LON
            home(lon, target, (lat, target)).start()
            return carry

        lax.fori_loop(1, N_LON, own, 0)
        at = pl.ds(pl.multiple_of(place(lon) * BLOCK, 8), BLOCK)
        returned[pl.ds(pl.multiple_of(lon * BLOCK, 8), BLOCK), :] = sent_back[at, :]

    @pl.when(lends)
    def _():
        wait_for(gathered, N_LON, go_recv)
        circle(other * ROWS + (OWN + lon) // 3)

        def away(i, carry):
            target = (lon + i) % N_LON
            home(OWN + lon, target, (other, target)).start()
            return carry

        lax.fori_loop(0, N_LON, away, 0)

    def update(source):
        def whole(t, carry):
            at = pl.ds(pl.multiple_of(t * LANES, LANES), LANES)
            step = [source[pl.ds(f * TILES + t, ROWS, stride=3 * TILES), :] for f in range(3)]
            hv[:, at] = hv[:, at] + TIME_STEP * step[0]
            wv[0, :, at] = wv[0, :, at] + TIME_STEP * step[1]
            wv[1, :, at] = wv[1, :, at] + TIME_STEP * step[2]
            return carry

        lax.fori_loop(0, FULL, whole, 0)
        at = pl.ds(FULL * LANES, TAIL)
        step = [source[pl.ds(f * TILES + FULL, ROWS, stride=3 * TILES), :][:, :TAIL] for f in range(3)]
        hv[:, at] = hv[:, at] + TIME_STEP * step[0]
        wv[0, :, at] = wv[0, :, at] + TIME_STEP * step[1]
        wv[1, :, at] = wv[1, :, at] + TIME_STEP * step[2]

    @pl.when(polar)
    def _():
        wait_for(returned, PAIRS - 1, back_recv)
        update(returned)

    @pl.when(jnp.logical_not(polar))
    def _():
        update(tend)

    stores += [
        pltpu.make_async_copy(wv, winds_out, out_sem.at[1]),
        pltpu.make_async_copy(hv, thick_out, out_sem.at[2]),
    ]
    stores[1].start()
    stores[2].start()
    halos[2].wait_send()
    halos[3].wait_send()

    @pl.when(polar)
    def _():
        wait_for(tend, PAIRS - 1, go_send)
        wait_for(sent_back, N_LON - 1, back_send)

    @pl.when(lends)
    def _():
        wait_for(sent_back, N_LON, back_send)

    for store in stores:
        store.wait()


def local(winds, thickness, tracers, cutoff):
    fore, twiddle, mix, unmix, back = filter_tables()
    anywhere = pl.BlockSpec(memory_space=pl.ANY)
    scalar = pl.BlockSpec(memory_space=pltpu.SMEM)
    side = pltpu.VMEM((48, LANES), F32)
    dma = pltpu.SemaphoreType.DMA
    return pl.pallas_call(
        kernel,
        out_shape=(
            jax.ShapeDtypeStruct((2, ROWS, WIDE), F32),
            jax.ShapeDtypeStruct((ROWS, WIDE), F32),
            jax.ShapeDtypeStruct((3, ROWS, WIDE), BF16),
        ),
        in_specs=[scalar, scalar] + [anywhere] * 8,
        out_specs=(anywhere,) * 3,
        scratch_shapes=[
            pltpu.VMEM((2, ROWS, WIDE), F32),
            pltpu.VMEM((ROWS, WIDE), F32),
            pltpu.VMEM((3, ROWS, WIDE), BF16),
            pltpu.VMEM((3, ROWS, WIDE), BF16),
            pltpu.VMEM(((ROWS + 2) * SLOT, LANES), F32),
            side, side, side, side,
            pltpu.VMEM((PAIRS * BLOCK, LANES), F32),
            pltpu.VMEM((N_LON * BLOCK, LANES), F32),
            pltpu.VMEM((N_LON * BLOCK, LANES), F32),
            pltpu.VMEM((PAIRS * BLOCK, LANES), F32),
            pltpu.VMEM((PAIRS * BLOCK, LANES), F32),
            pltpu.VMEM(fore.shape, BF16),
            pltpu.VMEM(twiddle.shape, F32),
            pltpu.VMEM(mix.shape, BF16),
            pltpu.VMEM(unmix.shape, BF16),
            pltpu.VMEM(back.shape, BF16),
            dma((3,)), dma((5,)), dma((3,)), dma((4,)), dma((4,)), dma, dma, dma, dma,
        ],
        compiler_params=pltpu.CompilerParams(
            collective_id=0, has_side_effects=True, vmem_limit_bytes=40 * 1024 * 1024
        ),
        name="substep",
    )(cutoff, geometry(), winds, thickness, tracers, fore, twiddle, mix, unmix, back)


def solution(mesh):
    in_specs = (P(None, "lat", "lon"), P("lat", "lon"), P(None, "lat", "lon"), P())
    out_specs = (P(None, "lat", "lon"), P("lat", "lon"), P(None, "lat", "lon"))
    return jax.shard_map(local, mesh=mesh, in_specs=in_specs, out_specs=out_specs, check_vma=False)
```

```python
import functools
import math

import jax
import jax.numpy as jnp
import numpy as np
from jax import lax
from jax.experimental import pallas as pl
from jax.experimental.pallas import tpu as pltpu
from jax.sharding import PartitionSpec as P

MESH = pl.DeviceIdType.MESH
F32 = jnp.float32
BF16 = jnp.bfloat16

LEVELS = 16
NLAT = 288
NLON = 2880
POLAR = 48
TIME_STEP = 0.05
DIFFUSION = 0.5
RATIO = 2.0 * NLAT / NLON

N_LAT = 32
N_LON = 16
ROWS = NLAT // N_LAT
COLS = NLON // N_LON
WIDE = COLS * LEVELS

LANES = 128
PER = LANES // LEVELS
TILES = 24
FULL = WIDE // LANES
TAIL = WIDE - FULL * LANES
FIELDS = 6
SLOT = FIELDS * TILES
EDGE = 5 * TILES
PAIRS = 3 * ROWS
BLOCK = TILES
OWN = N_LON
AWAY = PAIRS - OWN

BASE = NLON // PER
HALF = BASE // 2 + 1
FREQ = 184
VMEM_MIB = 63
SIDE = N_LON // 2 * TILES


def geometry():
    row = np.arange(NLAT, dtype=np.float64)
    centre = (row + 0.5) * (math.pi / NLAT) - math.pi / 2

    def face(index):
        inside = (index >= 0) & (index < NLAT - 1)
        return np.where(inside, np.sin((index + 1) * (math.pi / NLAT)), 0.0)

    table = np.stack([1.0 / np.cos(centre), np.sin(centre), face(row), face(row - 1)], axis=1)
    return table.astype(np.float32).reshape(-1)


def split_table(table):
    high = table.astype(np.float32).astype(jnp.bfloat16)
    low = (table - high.astype(np.float64)).astype(np.float32).astype(jnp.bfloat16)
    return np.concatenate([high, low], axis=0)


def filter_tables():
    turn = 2.0 * math.pi
    freq = np.arange(FREQ)
    live = (freq < HALF).astype(np.float64)
    sector, tile = (a.reshape(-1) for a in np.meshgrid(np.arange(N_LON // 2), np.arange(TILES), indexing="ij"))
    used = (tile * PER < COLS).astype(np.float64)
    place = 2 * COLS * sector // PER + tile
    angle = turn * ((freq[:, None] * place[None, :]) % BASE) / BASE
    weight = live[:, None] * used[None, :]
    fore = np.concatenate([np.cos(angle) * weight, -np.sin(angle) * weight], axis=0)
    twice = np.where((freq == 0) | (freq == HALF - 1), 1.0, 2.0) / NLON
    back = np.concatenate([np.cos(angle) * weight * twice[:, None], -np.sin(angle) * weight * twice[:, None]], axis=0).T

    lane = np.arange(2 * LANES)
    shift = lane % LANES // LEVELS + COLS * (lane // LANES)
    angle = turn * ((freq[:, None] * shift[None, :]) % NLON) / NLON
    twiddle = np.concatenate([np.cos(angle), np.sin(angle)], axis=0).astype(np.float32)

    out = np.arange(LANES)
    angle = turn * ((BASE * shift[:, None] * (out // LEVELS)[None, :]) % NLON) / NLON
    same = (lane % LEVELS)[:, None] == (out % LEVELS)[None, :]
    cosine, sine = np.cos(angle) * same, np.sin(angle) * same
    mix = np.concatenate(
        [np.concatenate([cosine, -sine], axis=1), np.concatenate([sine, cosine], axis=1)], axis=0
    )
    return split_table(fore), twiddle, split_table(mix), split_table(mix.T), split_table(back)


def split(value):
    high = value.astype(BF16)
    low = (value - high.astype(F32)).astype(BF16)
    return high, low


def dot(a, b):
    return jnp.dot(a, b, preferred_element_type=F32)


def table_left(table, rows, value):
    high, low = split(value)
    first = table[pl.ds(0, rows), :]
    return dot(first, high) + dot(first, low) + dot(table[pl.ds(rows, rows), :], high)


def table_right(value, table, rows):
    high, low = split(value)
    first = table[pl.ds(0, rows), :]
    return dot(high, first) + dot(low, first) + dot(high, table[pl.ds(rows, rows), :])


def eastward(value):
    lane = lax.broadcasted_iota(jnp.int32, (TILES, LANES), 1)
    here = pltpu.roll(value, LANES - LEVELS, 1)
    return jnp.where(lane < LANES - LEVELS, here, pltpu.roll(here, TILES - 1, 0))


def westward(value):
    lane = lax.broadcasted_iota(jnp.int32, (TILES, LANES), 1)
    here = pltpu.roll(value, LEVELS, 1)
    return jnp.where(lane >= LEVELS, here, pltpu.roll(here, 1, 0))


def kernel(
    cut, geo, winds_in, thick_in, mass_in, fore_in, twiddle_in, mix_in, unmix_in, back_in,
    returned, mass,
    wv, hv, qv, cells, to_east, to_west, from_west, from_east, tend, gathered, sent_back,
    fore, twiddle, mix, unmix, back,
    in_sem, table_sem, halo_send, halo_recv, go_send, go_recv, back_send, back_recv,
):
    lat = lax.axis_index("lat")
    lon = lax.axis_index("lon")
    polar_south = lat * ROWS < POLAR
    polar_north = (lat + 1) * ROWS > NLAT - POLAR
    polar = jnp.logical_or(polar_south, polar_north)
    other = (lat + N_LAT // 2) % N_LAT
    other_polar = jnp.logical_or(other * ROWS < POLAR, (other + 1) * ROWS > NLAT - POLAR)
    lends = jnp.logical_and(other_polar, lon < AWAY)

    loads = [
        pltpu.make_async_copy(winds_in, wv, in_sem.at[0]),
        pltpu.make_async_copy(thick_in, hv, in_sem.at[1]),
        pltpu.make_async_copy(mass_in, qv, in_sem.at[2]),
    ]
    for load in loads:
        load.start()
    tables = [
        pltpu.make_async_copy(source, target, table_sem.at[i])
        for i, (source, target) in enumerate(
            ((fore_in, fore), (twiddle_in, twiddle), (mix_in, mix), (unmix_in, unmix), (back_in, back))
        )
    ]
    for load in tables:
        load.start()

    east = (lat, (lon + 1) % N_LON)
    west = (lat, (lon + N_LON - 1) % N_LON)
    below = (lat + N_LAT - 1) // N_LAT
    above = 1 - lat // (N_LAT - 1)
    south = (lat - below, (lon + (1 - below) * (N_LON // 2)) % N_LON)
    north = (lat + above, (lon + (1 - above) * (N_LON // 2)) % N_LON)

    barrier = pltpu.get_barrier_semaphore()

    def greet(device):
        pl.semaphore_signal(barrier, inc=1, device_id=device, device_id_type=MESH)

    for device in (east, west, south, north):
        greet(device)

    @pl.when(polar)
    def _():
        lax.fori_loop(1, N_LON, lambda i, c: (greet((lat, (lon + i) % N_LON)), c)[1], 0)
        lax.fori_loop(0, AWAY, lambda i, c: (greet((other, i)), c)[1], 0)

    @pl.when(lends)
    def _():
        lax.fori_loop(0, N_LON, lambda i, c: (greet((other, i)), c)[1], 0)

    for load in loads:
        load.wait()

    def padded(value):
        return jnp.concatenate([value, jnp.zeros((value.shape[0], LANES - TAIL), F32)], axis=1)

    def place_row(j, carry):
        start = (j + 1) * SLOT
        for t in range(FULL + 1):
            at = pl.ds(t * LANES, LANES if t < FULL else TAIL)
            wind, ratio = wv[j, :, at], qv[j, :, at].astype(F32)
            if t == FULL:
                wind, ratio = padded(wind), padded(ratio)
            cells[pl.ds(start + t, 2, stride=TILES), :] = wind
            cells[pl.ds(start + 3 * TILES + t, 3, stride=TILES), :] = ratio
        return carry

    lax.fori_loop(0, ROWS, place_row, 0)
    for t in range(FULL + 1):
        value = hv[:, pl.ds(t * LANES, LANES if t < FULL else TAIL)]
        cells[pl.ds(SLOT + 2 * TILES + t, ROWS, stride=SLOT), :] = value if t < FULL else padded(value)

    sides = (0, 2, 3, 4, 5)
    for i, f in enumerate(sides):
        first = cells[pl.ds(SLOT + f * TILES, ROWS, stride=SLOT), :]
        last = cells[pl.ds(SLOT + f * TILES + FULL, ROWS, stride=SLOT), :]
        to_west[pl.ds(i * ROWS, ROWS), :] = pltpu.roll(first, TAIL, 1)
        to_east[pl.ds(i * ROWS, ROWS), :] = pltpu.roll(last, LANES - TAIL, 1)

    @pl.when(polar)
    def _():
        pl.semaphore_wait(barrier, 4 + N_LON - 1 + AWAY)

    @pl.when(lends)
    def _():
        pl.semaphore_wait(barrier, 4 + N_LON)

    @pl.when(jnp.logical_not(jnp.logical_or(polar, lends)))
    def _():
        pl.semaphore_wait(barrier, 4)

    south_slot = below * (ROWS + 1)
    north_slot = (1 - above) * (ROWS + 1)

    def edge(slot):
        return cells.at[pl.ds(pl.multiple_of(slot * SLOT + TILES, 8), EDGE), :]

    halos = [
        pltpu.make_async_remote_copy(
            edge(1), edge(south_slot), halo_send.at[0], halo_recv.at[below], device_id=south, device_id_type=MESH
        ),
        pltpu.make_async_remote_copy(
            edge(ROWS), edge(north_slot), halo_send.at[1], halo_recv.at[1 - above],
            device_id=north, device_id_type=MESH,
        ),
        pltpu.make_async_remote_copy(
            to_east, from_west, halo_send.at[2], halo_recv.at[2], device_id=east, device_id_type=MESH
        ),
        pltpu.make_async_remote_copy(
            to_west, from_east, halo_send.at[3], halo_recv.at[3], device_id=west, device_id_type=MESH
        ),
    ]
    for halo in halos:
        halo.start()
    pltpu.make_async_copy(edge(0), edge(0), halo_recv.at[0]).wait()
    pltpu.make_async_copy(edge(ROWS + 1), edge(ROWS + 1), halo_recv.at[1]).wait()
    pltpu.make_async_copy(from_west, from_west, halo_recv.at[2]).wait()
    pltpu.make_async_copy(from_east, from_east, halo_recv.at[3]).wait()
    halos[0].wait_send()
    halos[1].wait_send()

    lane = lax.broadcasted_iota(jnp.int32, (ROWS, LANES), 1)
    for i, f in enumerate(sides):
        at = pl.ds(SLOT + f * TILES + FULL, ROWS, stride=SLOT)
        here = from_east[pl.ds(i * ROWS, ROWS), :]
        cells[at, :] = jnp.where((lane >= TAIL) & (lane < TAIL + LEVELS), here, cells[at, :])
        at = pl.ds(SLOT + f * TILES + FULL + 1, ROWS, stride=SLOT)
        here = from_west[pl.ds(i * ROWS, ROWS), :]
        cells[at, :] = jnp.where(lane >= LANES - LEVELS, here, 0.0)

    @pl.when(lat == 0)
    def _():
        at = pl.ds(TILES, TILES)
        cells[at, :] = -cells[at, :]

    @pl.when(lat == N_LAT - 1)
    def _():
        at = pl.ds((ROWS + 1) * SLOT + TILES, TILES)
        cells[at, :] = -cells[at, :]

    def row(slot, field):
        return cells[pl.ds(pl.multiple_of(slot * SLOT + field * TILES, 8), TILES), :]

    def scalars(j):
        at = (lat * ROWS + j) * 4
        return geo[at], geo[at + 1], geo[at + 2], geo[at + 3]

    flat = lax.broadcasted_iota(jnp.int32, (TILES, LANES), 0) * LANES + lax.broadcasted_iota(
        jnp.int32, (TILES, LANES), 1
    )
    valid = flat < WIDE

    def fluxes(j, cos_north, cos_south):
        h, h_n, h_s = row(j + 1, 2), row(j + 2, 2), row(j, 2)
        v, v_n, v_s = row(j + 1, 1), row(j + 2, 1), row(j, 1)
        u = row(j + 1, 0)
        h_e, h_w = eastward(h), westward(h)
        flux_e = 0.5 * (u + eastward(u)) * (0.5 * (h + h_e))
        flux_w = 0.5 * (westward(u) + u) * (0.5 * (h_w + h))
        flux_n = 0.5 * (v + v_n) * (0.5 * (h + h_n)) * cos_north
        flux_s = 0.5 * (v_s + v) * (0.5 * (h_s + h)) * cos_south
        return h, u, v, h_e, h_w, h_n, h_s, flux_e, flux_w, flux_n, flux_s

    def tendency(j, carry):
        inverse, sine, cos_north, cos_south = scalars(j)
        h, u, v, h_e, h_w, h_n, h_s, flux_e, flux_w, flux_n, flux_s = fluxes(j, cos_north, cos_south)
        values = (
            -((flux_e - flux_w) + RATIO * (flux_n - flux_s)) * inverse,
            sine * v - (h_e - h_w) * (0.5 * inverse),
            -sine * u - RATIO * (h_n - h_s) * 0.5,
        )
        for f, value in enumerate(values):
            at = pl.ds(pl.multiple_of((j * 3 + f) * BLOCK, 8), BLOCK)
            tend[at, :] = jnp.where(valid, value, 0.0)
        return carry

    lax.fori_loop(0, ROWS, tendency, 0)

    def block(ref, index):
        return ref.at[pl.ds(pl.multiple_of(index * BLOCK, 8), BLOCK), :]

    def place(sector):
        return (sector % 2) * (N_LON // 2) + sector // 2

    def go(pair, device):
        return pltpu.make_async_remote_copy(
            block(tend, pair), block(gathered, place(lon)), go_send, go_recv, device_id=device, device_id_type=MESH
        )

    @pl.when(polar)
    def _():
        def own(i, carry):
            target = (lon + i) % N_LON
            go(target, (lat, target)).start()
            return carry

        def away(i, carry):
            target = (lon + i) % AWAY
            go(OWN + target, (other, target)).start()
            return carry

        lax.fori_loop(0, AWAY, away, 0)
        lax.fori_loop(1, N_LON, own, 0)
        at = pl.ds(pl.multiple_of(place(lon) * BLOCK, 8), BLOCK)
        gathered[at, :] = tend[pl.ds(pl.multiple_of(lon * BLOCK, 8), BLOCK), :]

    def tracer(j, carry):
        inverse, sine, cos_north, cos_south = scalars(j)
        h, u, v, h_e, h_w, h_n, h_s, flux_e, flux_w, flux_n, flux_s = fluxes(j, cos_north, cos_south)
        for c in range(3):
            q, q_n, q_s = row(j + 1, 3 + c), row(j + 2, 3 + c), row(j, 3 + c)
            q_e, q_w = eastward(q), westward(q)
            zonal = flux_e * (0.5 * (q + q_e)) - flux_w * (0.5 * (q_w + q))
            merid = flux_n * (0.5 * (q + q_n)) - flux_s * (0.5 * (q_s + q))
            flux = (zonal + RATIO * merid) * inverse
            laplace = (q_e + q_w) + (q_n + q_s) - 4.0 * q
            at = pl.ds(pl.multiple_of((j * 3 + c) * TILES, 8), TILES)
            mass[at, :] = h * q + TIME_STEP * (DIFFUSION * laplace - flux)
        return carry

    lax.fori_loop(0, ROWS, tracer, 0)

    for load in tables:
        load.wait()

    def circle(pair_row):
        cutoff = cut[pair_row]
        data = jnp.concatenate([gathered[pl.ds(0, SIDE), :], gathered[pl.ds(SIDE, SIDE), :]], axis=1)
        lines = table_left(fore, 2 * FREQ, data)
        real, imag = lines[:FREQ], lines[FREQ:]
        cosine, sine = twiddle[pl.ds(0, FREQ), :], twiddle[pl.ds(FREQ, FREQ), :]
        turned = jnp.concatenate([real * cosine + imag * sine, imag * cosine - real * sine], axis=1)
        spectrum = table_right(turned, mix, 4 * LANES)
        wave = lax.broadcasted_iota(jnp.int32, (FREQ, 2 * LANES), 0) + BASE * (
            lax.broadcasted_iota(jnp.int32, (FREQ, 2 * LANES), 1) % LANES // LEVELS
        )
        wave = jnp.minimum(wave, NLON - wave)
        spectrum = jnp.where(wave <= cutoff, spectrum, 0.0)
        lines = table_right(spectrum, unmix, 2 * LANES)
        real, imag = lines[:, : 2 * LANES], lines[:, 2 * LANES :]
        turned = jnp.concatenate([real * cosine - imag * sine, real * sine + imag * cosine], axis=0)
        result = table_left(back, SIDE, turned)
        sent_back[pl.ds(0, SIDE), :] = result[:, :LANES]
        sent_back[pl.ds(SIDE, SIDE), :] = result[:, LANES:]

    def home(pair, sector, device):
        return pltpu.make_async_remote_copy(
            block(sent_back, place(sector)), block(returned, pair), back_send, back_recv,
            device_id=device, device_id_type=MESH,
        )

    def total(ref, blocks):
        return ref.at[pl.ds(0, blocks * BLOCK), :]

    def wait_for(ref, blocks, sem):
        pltpu.make_async_copy(total(ref, blocks), total(ref, blocks), sem).wait()

    @pl.when(polar)
    def _():
        wait_for(gathered, N_LON - 1, go_recv)
        circle(lat * ROWS + lon // 3)

        def own(i, carry):
            target = (lon + i) % N_LON
            home(lon, target, (lat, target)).start()
            return carry

        lax.fori_loop(1, N_LON, own, 0)
        at = pl.ds(pl.multiple_of(place(lon) * BLOCK, 8), BLOCK)
        returned[pl.ds(pl.multiple_of(lon * BLOCK, 8), BLOCK), :] = sent_back[at, :]

    @pl.when(lends)
    def _():
        wait_for(gathered, N_LON, go_recv)
        circle(other * ROWS + (OWN + lon) // 3)

        def away(i, carry):
            target = (lon + i) % N_LON
            home(OWN + lon, target, (other, target)).start()
            return carry

        lax.fori_loop(0, N_LON, away, 0)

    @pl.when(jnp.logical_not(polar))
    def _():
        returned[...] = tend[...]

    halos[2].wait_send()
    halos[3].wait_send()

    @pl.when(polar)
    def _():
        wait_for(tend, PAIRS - 1, go_send)
        wait_for(sent_back, N_LON - 1, back_send)
        wait_for(returned, PAIRS - 1, back_recv)

    @pl.when(lends)
    def _():
        wait_for(sent_back, N_LON, back_send)


def finish(winds, thick, steps, mass, winds_out, thick_out, mass_out):
    def one_row(j, carry):
        start = j * 3 * TILES
        for t in range(FULL + 1):
            width = LANES if t < FULL else TAIL
            at = pl.ds(t * LANES, width)
            step = steps[pl.ds(start + TILES + t, 2, stride=TILES), :]
            winds_out[j, :, at] = winds[j, :, at] + TIME_STEP * step[:, :width]
            mass_out[j, :, at] = mass[pl.ds(start + t, 3, stride=TILES), :][:, :width].astype(BF16)
        return carry

    lax.fori_loop(0, ROWS, one_row, 0)
    for t in range(FULL + 1):
        width = LANES if t < FULL else TAIL
        at = pl.ds(t * LANES, width)
        thick_out[:, at] = thick[:, at] + TIME_STEP * steps[pl.ds(t, ROWS, stride=3 * TILES), :][:, :width]


def local(winds, thickness, tracers, cutoff):
    fore, twiddle, mix, unmix, back = filter_tables()
    anywhere = pl.BlockSpec(memory_space=pl.ANY)
    scalar = pl.BlockSpec(memory_space=pltpu.SMEM)
    whole = pl.BlockSpec(memory_space=pltpu.VMEM)
    side = pltpu.VMEM((48, LANES), F32)
    dma = pltpu.SemaphoreType.DMA
    rows = jax.ShapeDtypeStruct((PAIRS * BLOCK, LANES), F32)
    winds = jnp.transpose(winds, (1, 0, 2))
    tracers = jnp.transpose(tracers, (1, 0, 2))
    steps, mass = pl.pallas_call(
        kernel,
        out_shape=(rows, rows),
        in_specs=[scalar, scalar] + [anywhere] * 8,
        out_specs=(whole, whole),
        scratch_shapes=[
            pltpu.VMEM((ROWS, 2, WIDE), F32),
            pltpu.VMEM((ROWS, WIDE), F32),
            pltpu.VMEM((ROWS, 3, WIDE), BF16),
            pltpu.VMEM(((ROWS + 2) * SLOT, LANES), F32),
            side, side, side, side,
            pltpu.VMEM((PAIRS * BLOCK, LANES), F32),
            pltpu.VMEM((N_LON * BLOCK, LANES), F32),
            pltpu.VMEM((N_LON * BLOCK, LANES), F32),
            pltpu.VMEM(fore.shape, BF16),
            pltpu.VMEM(twiddle.shape, F32),
            pltpu.VMEM(mix.shape, BF16),
            pltpu.VMEM(unmix.shape, BF16),
            pltpu.VMEM(back.shape, BF16),
            dma((3,)), dma((5,)), dma((4,)), dma((4,)), dma, dma, dma, dma,
        ],
        compiler_params=pltpu.CompilerParams(
            collective_id=0, has_side_effects=True, vmem_limit_bytes=VMEM_MIB * 1024 * 1024
        ),
        name="substep",
    )(cutoff, geometry(), winds, thickness, tracers, fore, twiddle, mix, unmix, back)
    new_winds, new_thickness, new_mass = pl.pallas_call(
        finish,
        out_shape=(
            jax.ShapeDtypeStruct((ROWS, 2, WIDE), F32),
            jax.ShapeDtypeStruct((ROWS, WIDE), F32),
            jax.ShapeDtypeStruct((ROWS, 3, WIDE), BF16),
        ),
        in_specs=[whole] * 4,
        out_specs=(whole,) * 3,
        name="finish",
    )(winds, thickness, steps, mass)
    return jnp.transpose(new_winds, (1, 0, 2)), new_thickness, jnp.transpose(new_mass, (1, 0, 2))


def solution(mesh):
    in_specs = (P(None, "lat", "lon"), P("lat", "lon"), P(None, "lat", "lon"), P())
    out_specs = (P(None, "lat", "lon"), P("lat", "lon"), P(None, "lat", "lon"))
    return jax.shard_map(local, mesh=mesh, in_specs=in_specs, out_specs=out_specs, check_vma=False)
```

```python
import functools
import math

import jax
import jax.numpy as jnp
import numpy as np
from jax import lax
from jax.experimental import pallas as pl
from jax.experimental.pallas import tpu as pltpu
from jax.sharding import PartitionSpec as P

MESH = pl.DeviceIdType.MESH
F32 = jnp.float32
BF16 = jnp.bfloat16

LEVELS = 16
NLAT = 288
NLON = 2880
POLAR = 48
TIME_STEP = 0.05
DIFFUSION = 0.5
RATIO = 2.0 * NLAT / NLON

N_LAT = 32
N_LON = 16
ROWS = NLAT // N_LAT
COLS = NLON // N_LON
WIDE = COLS * LEVELS

LANES = 128
PER = LANES // LEVELS
TILES = 24
FULL = WIDE // LANES
TAIL = WIDE - FULL * LANES
FIELDS = 6
SLOT = FIELDS * TILES
EDGE = 5 * TILES
PAIRS = 3 * ROWS
BLOCK = FULL + 1
OWN = 14
AWAY = PAIRS - OWN

BASE = NLON // PER
HALF = BASE // 2 + 1
FREQ = 184
VMEM_MIB = 63
SIDE = N_LON // 2 * TILES


def geometry():
    row = np.arange(NLAT, dtype=np.float64)
    centre = (row + 0.5) * (math.pi / NLAT) - math.pi / 2

    def face(index):
        inside = (index >= 0) & (index < NLAT - 1)
        return np.where(inside, np.sin((index + 1) * (math.pi / NLAT)), 0.0)

    table = np.stack([1.0 / np.cos(centre), np.sin(centre), face(row), face(row - 1)], axis=1)
    return table.astype(np.float32).reshape(-1)


def split_table(table):
    high = table.astype(np.float32).astype(jnp.bfloat16)
    low = (table - high.astype(np.float64)).astype(np.float32).astype(jnp.bfloat16)
    return np.concatenate([high, low], axis=0)


def filter_tables():
    turn = 2.0 * math.pi
    freq = np.arange(FREQ)
    live = (freq < HALF).astype(np.float64)
    sector, tile = (a.reshape(-1) for a in np.meshgrid(np.arange(N_LON // 2), np.arange(TILES), indexing="ij"))
    used = (tile * PER < COLS).astype(np.float64)
    place = 2 * COLS * sector // PER + tile
    angle = turn * ((freq[:, None] * place[None, :]) % BASE) / BASE
    weight = live[:, None] * used[None, :]
    fore = np.concatenate([np.cos(angle) * weight, -np.sin(angle) * weight], axis=0)
    twice = np.where((freq == 0) | (freq == HALF - 1), 1.0, 2.0) / NLON
    back = np.concatenate([np.cos(angle) * weight * twice[:, None], -np.sin(angle) * weight * twice[:, None]], axis=0).T

    lane = np.arange(2 * LANES)
    shift = lane % LANES // LEVELS + COLS * (lane // LANES)
    angle = turn * ((freq[:, None] * shift[None, :]) % NLON) / NLON
    twiddle = np.concatenate([np.cos(angle), np.sin(angle)], axis=0).astype(np.float32)

    out = np.arange(LANES)
    angle = turn * ((BASE * shift[:, None] * (out // LEVELS)[None, :]) % NLON) / NLON
    same = (lane % LEVELS)[:, None] == (out % LEVELS)[None, :]
    cosine, sine = np.cos(angle) * same, np.sin(angle) * same
    mix = np.concatenate(
        [np.concatenate([cosine, -sine], axis=1), np.concatenate([sine, cosine], axis=1)], axis=0
    )
    return split_table(fore), twiddle, split_table(mix), split_table(mix.T), split_table(back)


def split(value):
    high = value.astype(BF16)
    low = (value - high.astype(F32)).astype(BF16)
    return high, low


def dot(a, b):
    return jnp.dot(a, b, preferred_element_type=F32)


def table_left(table, rows, value):
    high, low = split(value)
    first = table[pl.ds(0, rows), :]
    return dot(first, high) + dot(first, low) + dot(table[pl.ds(rows, rows), :], high)


def table_right(value, table, rows):
    high, low = split(value)
    first = table[pl.ds(0, rows), :]
    return dot(high, first) + dot(low, first) + dot(high, table[pl.ds(rows, rows), :])


def eastward(value):
    lane = lax.broadcasted_iota(jnp.int32, (TILES, LANES), 1)
    here = pltpu.roll(value, LANES - LEVELS, 1)
    return jnp.where(lane < LANES - LEVELS, here, pltpu.roll(here, TILES - 1, 0))


def westward(value):
    lane = lax.broadcasted_iota(jnp.int32, (TILES, LANES), 1)
    here = pltpu.roll(value, LEVELS, 1)
    return jnp.where(lane >= LEVELS, here, pltpu.roll(here, 1, 0))


def kernel(
    cut_in, geo_in, winds_in, thick_in, mass_in, fore_in, twiddle_in, mix_in, unmix_in, back_in,
    returned, mass,
    wv, hv, qv, cells, to_east, to_west, from_west, from_east, tend, gathered, sent_back,
    fore, twiddle, mix, unmix, back, cut, geo,
    in_sem, table_sem, halo_send, halo_recv, go_send, go_recv, back_send, back_recv,
):
    lat = lax.axis_index("lat")
    lon = lax.axis_index("lon")
    polar_south = lat * ROWS < POLAR
    polar_north = (lat + 1) * ROWS > NLAT - POLAR
    polar = jnp.logical_or(polar_south, polar_north)
    other = (lat + N_LAT // 2) % N_LAT
    other_polar = jnp.logical_or(other * ROWS < POLAR, (other + 1) * ROWS > NLAT - POLAR)
    works = jnp.logical_and(polar, lon < OWN)
    lends = jnp.logical_and(other_polar, lon < AWAY)

    east = (lat, (lon + 1) % N_LON)
    west = (lat, (lon + N_LON - 1) % N_LON)
    below = (lat + N_LAT - 1) // N_LAT
    above = 1 - lat // (N_LAT - 1)
    south = (lat - below, (lon + (1 - below) * (N_LON // 2)) % N_LON)
    north = (lat + above, (lon + (1 - above) * (N_LON // 2)) % N_LON)

    barrier = pltpu.get_barrier_semaphore()

    def greet(device):
        pl.semaphore_signal(barrier, inc=1, device_id=device, device_id_type=MESH)

    for device in (east, west, south, north):
        greet(device)

    @pl.when(polar)
    def _():
        lax.fori_loop(1, N_LON, lambda i, c: (greet((lat, (lon + i) % N_LON)), c)[1], 0)
        lax.fori_loop(0, AWAY, lambda i, c: (greet((other, i)), c)[1], 0)

    @pl.when(lends)
    def _():
        lax.fori_loop(0, N_LON, lambda i, c: (greet((other, i)), c)[1], 0)

    loads = [
        pltpu.make_async_copy(winds_in, wv, in_sem.at[0]),
        pltpu.make_async_copy(thick_in, hv, in_sem.at[1]),
        pltpu.make_async_copy(mass_in, qv, in_sem.at[2]),
        pltpu.make_async_copy(geo_in, geo, in_sem.at[3]),
        pltpu.make_async_copy(cut_in, cut, in_sem.at[4]),
    ]
    for load in loads:
        load.start()
    for load in loads:
        load.wait()
    tables = [
        pltpu.make_async_copy(source, target, table_sem.at[i])
        for i, (source, target) in enumerate(
            ((fore_in, fore), (twiddle_in, twiddle), (mix_in, mix), (unmix_in, unmix), (back_in, back))
        )
    ]
    for load in tables:
        load.start()

    def padded(value):
        return jnp.concatenate([value, jnp.zeros((value.shape[0], LANES - TAIL), F32)], axis=1)

    def place_row(j, carry):
        start = (j + 1) * SLOT
        for t in range(FULL + 1):
            at = pl.ds(t * LANES, LANES if t < FULL else TAIL)
            wind, ratio = wv[j, :, at], qv[j, :, at].astype(F32)
            if t == FULL:
                wind, ratio = padded(wind), padded(ratio)
            cells[pl.ds(start + t, 2, stride=TILES), :] = wind
            cells[pl.ds(start + 3 * TILES + t, 3, stride=TILES), :] = ratio
        cells[pl.ds(start + FULL + 1, FIELDS, stride=TILES), :] = jnp.zeros((FIELDS, LANES), F32)
        return carry

    lax.fori_loop(0, ROWS, place_row, 0)
    for t in range(FULL + 1):
        value = hv[:, pl.ds(t * LANES, LANES if t < FULL else TAIL)]
        cells[pl.ds(SLOT + 2 * TILES + t, ROWS, stride=SLOT), :] = value if t < FULL else padded(value)

    sides = (0, 2, 3, 4, 5)
    for i, f in enumerate(sides):
        first = cells[pl.ds(SLOT + f * TILES, ROWS, stride=SLOT), :]
        last = cells[pl.ds(SLOT + f * TILES + FULL, ROWS, stride=SLOT), :]
        to_west[pl.ds(i * ROWS, ROWS), :] = pltpu.roll(first, TAIL, 1)
        to_east[pl.ds(i * ROWS, ROWS), :] = pltpu.roll(last, LANES - TAIL, 1)

    gathered[pl.ds(FULL + 1, N_LON, stride=TILES), :] = jnp.zeros((N_LON, LANES), F32)

    def row(slot, field):
        return cells[pl.ds(pl.multiple_of(slot * SLOT + field * TILES, 8), TILES), :]

    def scalars(j):
        at = (lat * ROWS + j) * 4
        return geo[at], geo[at + 1], geo[at + 2], geo[at + 3]

    flat = lax.broadcasted_iota(jnp.int32, (TILES, LANES), 0) * LANES + lax.broadcasted_iota(
        jnp.int32, (TILES, LANES), 1
    )
    valid = flat < WIDE

    def fluxes(j, cos_north, cos_south):
        h, h_n, h_s = row(j + 1, 2), row(j + 2, 2), row(j, 2)
        v, v_n, v_s = row(j + 1, 1), row(j + 2, 1), row(j, 1)
        u = row(j + 1, 0)
        h_e, h_w = eastward(h), westward(h)
        flux_e = 0.5 * (u + eastward(u)) * (0.5 * (h + h_e))
        flux_w = 0.5 * (westward(u) + u) * (0.5 * (h_w + h))
        flux_n = 0.5 * (v + v_n) * (0.5 * (h + h_n)) * cos_north
        flux_s = 0.5 * (v_s + v) * (0.5 * (h_s + h)) * cos_south
        return h, u, v, h_e, h_w, h_n, h_s, flux_e, flux_w, flux_n, flux_s

    lane = lax.broadcasted_iota(jnp.int32, (ROWS, LANES), 1)

    def keep_row(j, f, target, value):
        at = pl.ds(pl.multiple_of((j * 3 + f) * TILES, 8), TILES)
        target[at, :] = jnp.where(valid, value, 0.0)

    def along(j):
        inverse, sine = scalars(j)[:2]
        h, v = row(j + 1, 2), row(j + 1, 1)
        return sine * v - (eastward(h) - westward(h)) * (0.5 * inverse)

    def tendency(j, target, both):
        inverse, sine, cos_north, cos_south = scalars(j)
        h, u, v, h_e, h_w, h_n, h_s, flux_e, flux_w, flux_n, flux_s = fluxes(j, cos_north, cos_south)
        keep_row(j, 0, target, -((flux_e - flux_w) + RATIO * (flux_n - flux_s)) * inverse)
        if both:
            keep_row(j, 1, target, sine * v - (h_e - h_w) * (0.5 * inverse))
        keep_row(j, 2, target, -sine * u - RATIO * (h_n - h_s) * 0.5)

    def corner():
        def column(field, tile, lanes):
            value = cells[pl.ds(SLOT + field * TILES + tile, ROWS, stride=SLOT), :]
            return pltpu.roll(value, lanes, 1)

        last = TAIL - LEVELS
        value = jnp.where(lane < TAIL + LEVELS, column(2, 0, TAIL), column(2, FULL, TAIL + LEVELS - last))
        value = jnp.where(lane < TAIL + 2 * LEVELS, value, column(0, 0, TAIL + 2 * LEVELS))
        return jnp.where(lane < TAIL + 3 * LEVELS, value, column(0, FULL, TAIL + 3 * LEVELS - last))

    @pl.when(polar)
    def _():
        lax.fori_loop(1, ROWS - 1, lambda j, c: (tendency(j, tend, True), c)[1], 0)
        for j in (0, ROWS - 1):
            keep_row(j, 1, tend, along(j))
        value = corner()
        at = pl.ds(TILES + FULL, ROWS, stride=3 * TILES)
        tend[at, :] = jnp.where(lane < TAIL, tend[at, :], value)
        at = pl.ds(3 * TILES + FULL, ROWS - 2, stride=3 * TILES)
        inner = slice(1, ROWS - 1)
        tend[at, :] = jnp.where(lane[inner] < TAIL, tend[at, :], value[inner])

    def block(ref, index):
        return ref.at[pl.ds(pl.multiple_of(index * TILES, 8), BLOCK), :]

    def place(sector):
        return (sector % 2) * (N_LON // 2) + sector // 2

    def go(pair, device):
        return pltpu.make_async_remote_copy(
            block(tend, pair), block(gathered, place(lon)), go_send, go_recv, device_id=device, device_id_type=MESH
        )

    @pl.when(polar)
    def _():
        pl.semaphore_wait(barrier, 4 + N_LON - 1 + AWAY)

    @pl.when(lends)
    def _():
        pl.semaphore_wait(barrier, 4 + N_LON)

    @pl.when(jnp.logical_not(jnp.logical_or(polar, lends)))
    def _():
        pl.semaphore_wait(barrier, 4)

    south_slot = below * (ROWS + 1)
    north_slot = (1 - above) * (ROWS + 1)

    def edge(slot):
        return cells.at[pl.ds(pl.multiple_of(slot * SLOT + TILES, 8), EDGE), :]

    halos = [
        pltpu.make_async_remote_copy(
            edge(1), edge(south_slot), halo_send.at[0], halo_recv.at[below], device_id=south, device_id_type=MESH
        ),
        pltpu.make_async_remote_copy(
            edge(ROWS), edge(north_slot), halo_send.at[1], halo_recv.at[1 - above],
            device_id=north, device_id_type=MESH,
        ),
        pltpu.make_async_remote_copy(
            to_east, from_west, halo_send.at[2], halo_recv.at[2], device_id=east, device_id_type=MESH
        ),
        pltpu.make_async_remote_copy(
            to_west, from_east, halo_send.at[3], halo_recv.at[3], device_id=west, device_id_type=MESH
        ),
    ]
    for halo in halos:
        halo.start()

    def rows_arrive():
        pltpu.make_async_copy(edge(0), edge(0), halo_recv.at[0]).wait()
        pltpu.make_async_copy(edge(ROWS + 1), edge(ROWS + 1), halo_recv.at[1]).wait()

        @pl.when(lat == 0)
        def _():
            at = pl.ds(TILES, TILES)
            cells[at, :] = -cells[at, :]

        @pl.when(lat == N_LAT - 1)
        def _():
            at = pl.ds((ROWS + 1) * SLOT + TILES, TILES)
            cells[at, :] = -cells[at, :]

    def send(pair):
        if pair < OWN:

            @pl.when(lon != pair)
            def _():
                go(pair, (lat, pair)).start()
        else:
            go(pair, (other, pair - OWN)).start()

    late = (0, 2, PAIRS - 3, PAIRS - 1)

    def is_early(pair):
        ready = pair != late[0]
        for other_pair in late[1:]:
            ready = jnp.logical_and(ready, pair != other_pair)
        return ready

    @pl.when(polar)
    def _():
        def early(i, carry):
            near = (lon + i) % N_LON

            @pl.when(jnp.logical_and(jnp.logical_and(near < OWN, near != lon), is_early(near)))
            def _():
                go(near, (lat, near)).start()

            far = (lon + i) % N_LON

            @pl.when(jnp.logical_and(far < AWAY, is_early(far + OWN)))
            def _():
                go(far + OWN, (other, far)).start()

            return carry

        lax.fori_loop(0, N_LON, early, 0)
        rows_arrive()
        for j in (0, ROWS - 1):
            tendency(j, tend, False)
        value = corner()
        for j in (0, ROWS - 1):
            at = pl.ds(3 * j * TILES + FULL, 1)
            tend[at, :] = jnp.where(lane[:1] < TAIL, tend[at, :], value[j : j + 1])
        for pair in late:
            send(pair)

    @pl.when(works)
    def _():
        at = pl.ds(pl.multiple_of(place(lon) * TILES, 8), BLOCK)
        gathered[at, :] = tend[pl.ds(pl.multiple_of(lon * TILES, 8), BLOCK), :]

    def complete(pair, lat_row):
        inverse = geo[lat_row * 4]
        first_at, last_at = pl.ds(0, N_LON, stride=TILES), pl.ds(FULL, N_LON, stride=TILES)
        first, last = gathered[first_at, :], gathered[last_at, :]
        spot = lax.broadcasted_iota(jnp.int32, (N_LON, LANES), 1)
        half = N_LON // 2
        after = jnp.concatenate([last[half:], pltpu.roll(last[:half], half - 1, 0)], axis=0)
        before = jnp.concatenate([pltpu.roll(last[half:], 1, 0), last[:half]], axis=0)

        def pick(value, part, to):
            return pltpu.roll(value, (LANES + to - TAIL - part * LEVELS) % LANES, 1)

        end = TAIL - LEVELS
        h_first, h_end, u_first, u_end = 0, 1, 2, 3
        field = pair % 3

        def put(east, west):
            gathered[last_at, :] = jnp.where(spot < end, last, jnp.where(spot < TAIL, last + east, 0.0))
            gathered[first_at, :] = jnp.where(spot < LEVELS, first + west, first)

        @pl.when(field == 0)
        def _():
            h, u = pick(last, h_end, end), pick(last, u_end, end)
            east = (u + pick(after, u_first, end)) * (h + pick(after, h_first, end)) - u * h
            h, u = pick(last, h_first, 0), pick(last, u_first, 0)
            west = (u + pick(before, u_end, 0)) * (h + pick(before, h_end, 0)) - u * h
            put(-0.25 * inverse * east, 0.25 * inverse * west)

        @pl.when(field == 1)
        def _():
            put(-0.5 * inverse * pick(after, h_first, end), 0.5 * inverse * pick(before, h_end, 0))

    def circle(pair, first_row):
        lat_row = first_row + pair // 3
        complete(pair, lat_row)
        cutoff = cut[lat_row]
        data = jnp.concatenate([gathered[pl.ds(0, SIDE), :], gathered[pl.ds(SIDE, SIDE), :]], axis=1)
        lines = table_left(fore, 2 * FREQ, data)
        real, imag = lines[:FREQ], lines[FREQ:]
        cosine, sine = twiddle[pl.ds(0, FREQ), :], twiddle[pl.ds(FREQ, FREQ), :]
        turned = jnp.concatenate([real * cosine + imag * sine, imag * cosine - real * sine], axis=1)
        spectrum = table_right(turned, mix, 4 * LANES)
        wave = lax.broadcasted_iota(jnp.int32, (FREQ, 2 * LANES), 0) + BASE * (
            lax.broadcasted_iota(jnp.int32, (FREQ, 2 * LANES), 1) % LANES // LEVELS
        )
        wave = jnp.minimum(wave, NLON - wave)
        spectrum = jnp.where(wave <= cutoff, spectrum, 0.0)
        lines = table_right(spectrum, unmix, 2 * LANES)
        real, imag = lines[:, : 2 * LANES], lines[:, 2 * LANES :]
        turned = jnp.concatenate([real * cosine - imag * sine, real * sine + imag * cosine], axis=0)
        result = table_left(back, SIDE, turned)
        sent_back[pl.ds(0, SIDE), :] = result[:, :LANES]
        sent_back[pl.ds(SIDE, SIDE), :] = result[:, LANES:]

    def home(pair, sector, device):
        return pltpu.make_async_remote_copy(
            block(sent_back, place(sector)), block(returned, pair), back_send, back_recv,
            device_id=device, device_id_type=MESH,
        )

    def total(ref, blocks):
        return ref.at[pl.ds(0, blocks * BLOCK), :]

    def wait_for(ref, blocks, sem):
        pltpu.make_async_copy(total(ref, blocks), total(ref, blocks), sem).wait()

    @pl.when(lends)
    def _():
        for load in tables:
            load.wait()
        wait_for(gathered, N_LON, go_recv)
        circle(OWN + lon, other * ROWS)

        def away(i, carry):
            target = (lon + i) % N_LON
            home(OWN + lon, target, (other, target)).start()
            return carry

        lax.fori_loop(0, N_LON, away, 0)

    @pl.when(jnp.logical_not(polar))
    def _():
        rows_arrive()

    pltpu.make_async_copy(from_west, from_west, halo_recv.at[2]).wait()
    pltpu.make_async_copy(from_east, from_east, halo_recv.at[3]).wait()
    halos[0].wait_send()
    halos[1].wait_send()
    for i, f in enumerate(sides):
        at = pl.ds(SLOT + f * TILES + FULL, ROWS, stride=SLOT)
        here = from_east[pl.ds(i * ROWS, ROWS), :]
        cells[at, :] = jnp.where((lane >= TAIL) & (lane < TAIL + LEVELS), here, cells[at, :])
        at = pl.ds(SLOT + f * TILES + FULL + 1, ROWS, stride=SLOT)
        here = from_west[pl.ds(i * ROWS, ROWS), :]
        cells[at, :] = jnp.where(lane >= LANES - LEVELS, here, 0.0)

    @pl.when(jnp.logical_not(polar))
    def _():
        lax.fori_loop(0, ROWS, lambda j, c: (tendency(j, returned, True), c)[1], 0)

    def tracer(j, carry):
        inverse, sine, cos_north, cos_south = scalars(j)
        h, u, v, h_e, h_w, h_n, h_s, flux_e, flux_w, flux_n, flux_s = fluxes(j, cos_north, cos_south)
        for c in range(3):
            q, q_n, q_s = row(j + 1, 3 + c), row(j + 2, 3 + c), row(j, 3 + c)
            q_e, q_w = eastward(q), westward(q)
            zonal = flux_e * (0.5 * (q + q_e)) - flux_w * (0.5 * (q_w + q))
            merid = flux_n * (0.5 * (q + q_n)) - flux_s * (0.5 * (q_s + q))
            flux = (zonal + RATIO * merid) * inverse
            laplace = (q_e + q_w) + (q_n + q_s) - 4.0 * q
            at = pl.ds(pl.multiple_of((j * 3 + c) * TILES, 8), TILES)
            mass[at, :] = h * q + TIME_STEP * (DIFFUSION * laplace - flux)
        return carry

    lax.fori_loop(0, ROWS, tracer, 0)

    @pl.when(jnp.logical_not(lends))
    def _():
        for load in tables:
            load.wait()

    @pl.when(works)
    def _():
        wait_for(gathered, N_LON - 1, go_recv)
        circle(lon, lat * ROWS)

        def own(i, carry):
            target = (lon + i) % N_LON
            home(lon, target, (lat, target)).start()
            return carry

        lax.fori_loop(1, N_LON, own, 0)
        at = pl.ds(pl.multiple_of(place(lon) * TILES, 8), BLOCK)
        returned[pl.ds(pl.multiple_of(lon * TILES, 8), BLOCK), :] = sent_back[at, :]

    halos[2].wait_send()
    halos[3].wait_send()

    @pl.when(works)
    def _():
        wait_for(tend, PAIRS - 1, go_send)
        wait_for(sent_back, N_LON - 1, back_send)
        wait_for(returned, PAIRS - 1, back_recv)

    @pl.when(jnp.logical_and(polar, lon >= OWN))
    def _():
        wait_for(tend, PAIRS, go_send)
        wait_for(returned, PAIRS, back_recv)

    @pl.when(lends)
    def _():
        wait_for(sent_back, N_LON, back_send)


def finish(winds, thick, steps, mass, winds_out, thick_out, mass_out):
    def one_row(j, carry):
        start = j * 3 * TILES
        for t in range(FULL + 1):
            width = LANES if t < FULL else TAIL
            at = pl.ds(t * LANES, width)
            step = steps[pl.ds(start + TILES + t, 2, stride=TILES), :]
            winds_out[j, :, at] = winds[j, :, at] + TIME_STEP * step[:, :width]
            mass_out[j, :, at] = mass[pl.ds(start + t, 3, stride=TILES), :][:, :width].astype(BF16)
        return carry

    lax.fori_loop(0, ROWS, one_row, 0)
    for t in range(FULL + 1):
        width = LANES if t < FULL else TAIL
        at = pl.ds(t * LANES, width)
        thick_out[:, at] = thick[:, at] + TIME_STEP * steps[pl.ds(t, ROWS, stride=3 * TILES), :][:, :width]


def local(winds, thickness, tracers, cutoff):
    fore, twiddle, mix, unmix, back = filter_tables()
    anywhere = pl.BlockSpec(memory_space=pl.ANY)
    whole = pl.BlockSpec(memory_space=pltpu.VMEM)
    side = pltpu.VMEM((48, LANES), F32)
    dma = pltpu.SemaphoreType.DMA
    rows = jax.ShapeDtypeStruct((PAIRS * TILES, LANES), F32)
    winds = jnp.transpose(winds, (1, 0, 2))
    tracers = jnp.transpose(tracers, (1, 0, 2))
    steps, mass = pl.pallas_call(
        kernel,
        out_shape=(rows, rows),
        in_specs=[anywhere] * 10,
        out_specs=(whole, whole),
        scratch_shapes=[
            pltpu.VMEM((ROWS, 2, WIDE), F32),
            pltpu.VMEM((ROWS, WIDE), F32),
            pltpu.VMEM((ROWS, 3, WIDE), BF16),
            pltpu.VMEM(((ROWS + 2) * SLOT, LANES), F32),
            side, side, side, side,
            pltpu.VMEM((PAIRS * TILES, LANES), F32),
            pltpu.VMEM((N_LON * TILES, LANES), F32),
            pltpu.VMEM((N_LON * TILES, LANES), F32),
            pltpu.VMEM(fore.shape, BF16),
            pltpu.VMEM(twiddle.shape, F32),
            pltpu.VMEM(mix.shape, BF16),
            pltpu.VMEM(unmix.shape, BF16),
            pltpu.VMEM(back.shape, BF16),
            pltpu.SMEM((NLAT,), jnp.int32),
            pltpu.SMEM((4 * NLAT,), F32),
            dma((5,)), dma((5,)), dma((4,)), dma((4,)), dma, dma, dma, dma,
        ],
        compiler_params=pltpu.CompilerParams(
            collective_id=0, has_side_effects=True, vmem_limit_bytes=VMEM_MIB * 1024 * 1024
        ),
        name="substep",
    )(cutoff, geometry(), winds, thickness, tracers, fore, twiddle, mix, unmix, back)
    new_winds, new_thickness, new_mass = pl.pallas_call(
        finish,
        out_shape=(
            jax.ShapeDtypeStruct((ROWS, 2, WIDE), F32),
            jax.ShapeDtypeStruct((ROWS, WIDE), F32),
            jax.ShapeDtypeStruct((ROWS, 3, WIDE), BF16),
        ),
        in_specs=[whole] * 4,
        out_specs=(whole,) * 3,
        name="finish",
    )(winds, thickness, steps, mass)
    return jnp.transpose(new_winds, (1, 0, 2)), new_thickness, jnp.transpose(new_mass, (1, 0, 2))


def solution(mesh):
    in_specs = (P(None, "lat", "lon"), P("lat", "lon"), P(None, "lat", "lon"), P())
    out_specs = (P(None, "lat", "lon"), P("lat", "lon"), P(None, "lat", "lon"))
    return jax.shard_map(local, mesh=mesh, in_specs=in_specs, out_specs=out_specs, check_vma=False)
```

```python
import functools
import math

import jax
import jax.numpy as jnp
import numpy as np
from jax import lax
from jax.experimental import pallas as pl
from jax.experimental.pallas import tpu as pltpu
from jax.sharding import PartitionSpec as P

MESH = pl.DeviceIdType.MESH
F32 = jnp.float32
BF16 = jnp.bfloat16

LEVELS = 16
NLAT = 288
NLON = 2880
POLAR = 48
TIME_STEP = 0.05
DIFFUSION = 0.5
RATIO = 2.0 * NLAT / NLON

N_LAT = 32
N_LON = 16
ROWS = NLAT // N_LAT
COLS = NLON // N_LON
WIDE = COLS * LEVELS

LANES = 128
PER = LANES // LEVELS
TILES = 24
FULL = WIDE // LANES
TAIL = WIDE - FULL * LANES
FIELDS = 6
SLOT = FIELDS * TILES
EDGE = 5 * TILES
PAIRS = 3 * ROWS
BLOCK = FULL + 1
OWN = N_LON
FAR = 12
AWAY = PAIRS - OWN

BASE = NLON // PER
HALF = BASE // 2 + 1
FREQ = 184
VMEM_MIB = 63
SIDE = N_LON // 2 * TILES


def geometry():
    row = np.arange(NLAT, dtype=np.float64)
    centre = (row + 0.5) * (math.pi / NLAT) - math.pi / 2

    def face(index):
        inside = (index >= 0) & (index < NLAT - 1)
        return np.where(inside, np.sin((index + 1) * (math.pi / NLAT)), 0.0)

    table = np.stack([1.0 / np.cos(centre), np.sin(centre), face(row), face(row - 1)], axis=1)
    return table.astype(np.float32).reshape(-1)


def split_table(table):
    high = table.astype(np.float32).astype(jnp.bfloat16)
    low = (table - high.astype(np.float64)).astype(np.float32).astype(jnp.bfloat16)
    return np.concatenate([high, low], axis=0)


def filter_tables():
    turn = 2.0 * math.pi
    freq = np.arange(FREQ)
    live = (freq < HALF).astype(np.float64)
    sector, tile = (a.reshape(-1) for a in np.meshgrid(np.arange(N_LON // 2), np.arange(TILES), indexing="ij"))
    used = (tile * PER < COLS).astype(np.float64)
    place = 2 * COLS * sector // PER + tile
    angle = turn * ((freq[:, None] * place[None, :]) % BASE) / BASE
    weight = live[:, None] * used[None, :]
    fore = np.concatenate([np.cos(angle) * weight, -np.sin(angle) * weight], axis=0)
    twice = np.where((freq == 0) | (freq == HALF - 1), 1.0, 2.0) / NLON
    back = np.concatenate([np.cos(angle) * weight * twice[:, None], -np.sin(angle) * weight * twice[:, None]], axis=0).T

    lane = np.arange(2 * LANES)
    shift = lane % LANES // LEVELS + COLS * (lane // LANES)
    angle = turn * ((freq[:, None] * shift[None, :]) % NLON) / NLON
    twiddle = np.concatenate([np.cos(angle), np.sin(angle)], axis=0).astype(np.float32)

    out = np.arange(LANES)
    angle = turn * ((BASE * shift[:, None] * (out // LEVELS)[None, :]) % NLON) / NLON
    same = (lane % LEVELS)[:, None] == (out % LEVELS)[None, :]
    cosine, sine = np.cos(angle) * same, np.sin(angle) * same
    mix = np.concatenate(
        [np.concatenate([cosine, -sine], axis=1), np.concatenate([sine, cosine], axis=1)], axis=0
    )
    return split_table(fore), twiddle, split_table(mix), split_table(mix.T), split_table(back)


def split(value):
    high = value.astype(BF16)
    low = (value - high.astype(F32)).astype(BF16)
    return high, low


def dot(a, b):
    return jnp.dot(a, b, preferred_element_type=F32)


def table_left(table, rows, value):
    high, low = split(value)
    first = table[pl.ds(0, rows), :]
    return dot(first, high) + dot(first, low) + dot(table[pl.ds(rows, rows), :], high)


def table_right(value, table, rows):
    high, low = split(value)
    first = table[pl.ds(0, rows), :]
    return dot(high, first) + dot(low, first) + dot(high, table[pl.ds(rows, rows), :])


def eastward(value):
    lane = lax.broadcasted_iota(jnp.int32, (TILES, LANES), 1)
    here = pltpu.roll(value, LANES - LEVELS, 1)
    return jnp.where(lane < LANES - LEVELS, here, pltpu.roll(here, TILES - 1, 0))


def westward(value):
    lane = lax.broadcasted_iota(jnp.int32, (TILES, LANES), 1)
    here = pltpu.roll(value, LEVELS, 1)
    return jnp.where(lane >= LEVELS, here, pltpu.roll(here, 1, 0))


def kernel(
    cut_in, geo_in, winds_in, thick_in, mass_in, fore_in, twiddle_in, mix_in, unmix_in, back_in,
    returned, mass,
    wv, hv, qv, cells, to_east, to_west, from_west, from_east, tend, gathered, sent_back,
    fore, twiddle, mix, unmix, back, cut, geo,
    in_sem, table_sem, halo_send, halo_recv, go_send, go_recv, back_send, back_recv,
):
    lat = lax.axis_index("lat")
    lon = lax.axis_index("lon")
    polar_south = lat * ROWS < POLAR
    polar_north = (lat + 1) * ROWS > NLAT - POLAR
    polar = jnp.logical_or(polar_south, polar_north)
    other = (lat + N_LAT // 2) % N_LAT
    other_polar = jnp.logical_or(other * ROWS < POLAR, (other + 1) * ROWS > NLAT - POLAR)
    lends = jnp.logical_and(other_polar, lon < AWAY)

    east = (lat, (lon + 1) % N_LON)
    west = (lat, (lon + N_LON - 1) % N_LON)
    below = (lat + N_LAT - 1) // N_LAT
    above = 1 - lat // (N_LAT - 1)
    south = (lat - below, (lon + (1 - below) * (N_LON // 2)) % N_LON)
    north = (lat + above, (lon + (1 - above) * (N_LON // 2)) % N_LON)

    barrier = pltpu.get_barrier_semaphore()

    def greet(device):
        pl.semaphore_signal(barrier, inc=1, device_id=device, device_id_type=MESH)

    for device in (east, west, south, north):
        greet(device)

    @pl.when(polar)
    def _():
        lax.fori_loop(1, N_LON, lambda i, c: (greet((lat, (lon + i) % N_LON)), c)[1], 0)
        lax.fori_loop(0, AWAY, lambda i, c: (greet((other, i)), c)[1], 0)

    @pl.when(lends)
    def _():
        lax.fori_loop(0, N_LON, lambda i, c: (greet((other, i)), c)[1], 0)

    loads = [
        pltpu.make_async_copy(winds_in, wv, in_sem.at[0]),
        pltpu.make_async_copy(thick_in, hv, in_sem.at[1]),
        pltpu.make_async_copy(mass_in, qv, in_sem.at[2]),
        pltpu.make_async_copy(geo_in, geo, in_sem.at[3]),
        pltpu.make_async_copy(cut_in, cut, in_sem.at[4]),
    ]
    for load in loads:
        load.start()
    for load in loads:
        load.wait()
    tables = [
        pltpu.make_async_copy(source, target, table_sem.at[i])
        for i, (source, target) in enumerate(
            ((fore_in, fore), (twiddle_in, twiddle), (mix_in, mix), (unmix_in, unmix), (back_in, back))
        )
    ]
    for load in tables:
        load.start()

    def padded(value):
        return jnp.concatenate([value, jnp.zeros((value.shape[0], LANES - TAIL), F32)], axis=1)

    def place_row(j, carry):
        start = (j + 1) * SLOT
        for t in range(FULL + 1):
            at = pl.ds(t * LANES, LANES if t < FULL else TAIL)
            wind, ratio = wv[j, :, at], qv[j, :, at].astype(F32)
            if t == FULL:
                wind, ratio = padded(wind), padded(ratio)
            cells[pl.ds(start + t, 2, stride=TILES), :] = wind
            cells[pl.ds(start + 3 * TILES + t, 3, stride=TILES), :] = ratio
        cells[pl.ds(start + FULL + 1, FIELDS, stride=TILES), :] = jnp.zeros((FIELDS, LANES), F32)
        return carry

    lax.fori_loop(0, ROWS, place_row, 0)
    for t in range(FULL + 1):
        value = hv[:, pl.ds(t * LANES, LANES if t < FULL else TAIL)]
        cells[pl.ds(SLOT + 2 * TILES + t, ROWS, stride=SLOT), :] = value if t < FULL else padded(value)

    sides = (0, 2, 3, 4, 5)
    for i, f in enumerate(sides):
        first = cells[pl.ds(SLOT + f * TILES, ROWS, stride=SLOT), :]
        last = cells[pl.ds(SLOT + f * TILES + FULL, ROWS, stride=SLOT), :]
        to_west[pl.ds(i * ROWS, ROWS), :] = pltpu.roll(first, TAIL, 1)
        to_east[pl.ds(i * ROWS, ROWS), :] = pltpu.roll(last, LANES - TAIL, 1)

    gathered[pl.ds(FULL + 1, N_LON, stride=TILES), :] = jnp.zeros((N_LON, LANES), F32)

    def row(slot, field):
        return cells[pl.ds(pl.multiple_of(slot * SLOT + field * TILES, 8), TILES), :]

    def scalars(j):
        at = (lat * ROWS + j) * 4
        return geo[at], geo[at + 1], geo[at + 2], geo[at + 3]

    flat = lax.broadcasted_iota(jnp.int32, (TILES, LANES), 0) * LANES + lax.broadcasted_iota(
        jnp.int32, (TILES, LANES), 1
    )
    valid = flat < WIDE

    def fluxes(j, cos_north, cos_south):
        h, h_n, h_s = row(j + 1, 2), row(j + 2, 2), row(j, 2)
        v, v_n, v_s = row(j + 1, 1), row(j + 2, 1), row(j, 1)
        u = row(j + 1, 0)
        h_e, h_w = eastward(h), westward(h)
        flux_e = 0.5 * (u + eastward(u)) * (0.5 * (h + h_e))
        flux_w = 0.5 * (westward(u) + u) * (0.5 * (h_w + h))
        flux_n = 0.5 * (v + v_n) * (0.5 * (h + h_n)) * cos_north
        flux_s = 0.5 * (v_s + v) * (0.5 * (h_s + h)) * cos_south
        return h, u, v, h_e, h_w, h_n, h_s, flux_e, flux_w, flux_n, flux_s

    lane = lax.broadcasted_iota(jnp.int32, (ROWS, LANES), 1)

    def keep_row(j, f, target, value):
        at = pl.ds(pl.multiple_of((j * 3 + f) * TILES, 8), TILES)
        target[at, :] = jnp.where(valid, value, 0.0)

    def along(j):
        inverse, sine = scalars(j)[:2]
        h, v = row(j + 1, 2), row(j + 1, 1)
        return sine * v - (eastward(h) - westward(h)) * (0.5 * inverse)

    def tendency(j, target, both):
        inverse, sine, cos_north, cos_south = scalars(j)
        h, u, v, h_e, h_w, h_n, h_s, flux_e, flux_w, flux_n, flux_s = fluxes(j, cos_north, cos_south)
        keep_row(j, 0, target, -((flux_e - flux_w) + RATIO * (flux_n - flux_s)) * inverse)
        if both:
            keep_row(j, 1, target, sine * v - (h_e - h_w) * (0.5 * inverse))
        keep_row(j, 2, target, -sine * u - RATIO * (h_n - h_s) * 0.5)

    def corner():
        def column(field, tile, lanes):
            value = cells[pl.ds(SLOT + field * TILES + tile, ROWS, stride=SLOT), :]
            return pltpu.roll(value, lanes, 1)

        last = TAIL - LEVELS
        value = jnp.where(lane < TAIL + LEVELS, column(2, 0, TAIL), column(2, FULL, TAIL + LEVELS - last))
        value = jnp.where(lane < TAIL + 2 * LEVELS, value, column(0, 0, TAIL + 2 * LEVELS))
        return jnp.where(lane < TAIL + 3 * LEVELS, value, column(0, FULL, TAIL + 3 * LEVELS - last))

    @pl.when(polar)
    def _():
        lax.fori_loop(1, ROWS - 1, lambda j, c: (tendency(j, tend, True), c)[1], 0)
        for j in (0, ROWS - 1):
            keep_row(j, 1, tend, along(j))
        value = corner()
        at = pl.ds(TILES + FULL, ROWS, stride=3 * TILES)
        tend[at, :] = jnp.where(lane < TAIL, tend[at, :], value)
        at = pl.ds(3 * TILES + FULL, ROWS - 2, stride=3 * TILES)
        inner = slice(1, ROWS - 1)
        tend[at, :] = jnp.where(lane[inner] < TAIL, tend[at, :], value[inner])

    def partner(i):
        ring = N_LON // 2
        k = ring - 1 - i // 2
        offset = (k + 1) // 2 * (2 * (k % 2) - 1)
        return (lon // ring + i % 2) % 2 * ring + (lon % ring + offset + ring) % ring

    def pair_of(i):
        return (2 * i + PAIRS - 4) % PAIRS

    def block(ref, index):
        return ref.at[pl.ds(pl.multiple_of(index * TILES, 8), BLOCK), :]

    def place(sector):
        return (sector % 2) * (N_LON // 2) + sector // 2

    def go(pair, device):
        return pltpu.make_async_remote_copy(
            block(tend, pair), block(gathered, place(lon)), go_send, go_recv, device_id=device, device_id_type=MESH
        )

    @pl.when(polar)
    def _():
        pl.semaphore_wait(barrier, 4 + N_LON - 1 + AWAY)

    @pl.when(lends)
    def _():
        pl.semaphore_wait(barrier, 4 + N_LON)

    @pl.when(jnp.logical_not(jnp.logical_or(polar, lends)))
    def _():
        pl.semaphore_wait(barrier, 4)

    south_slot = below * (ROWS + 1)
    north_slot = (1 - above) * (ROWS + 1)

    def edge(slot):
        return cells.at[pl.ds(pl.multiple_of(slot * SLOT + TILES, 8), EDGE), :]

    halos = [
        pltpu.make_async_remote_copy(
            edge(1), edge(south_slot), halo_send.at[0], halo_recv.at[below], device_id=south, device_id_type=MESH
        ),
        pltpu.make_async_remote_copy(
            edge(ROWS), edge(north_slot), halo_send.at[1], halo_recv.at[1 - above],
            device_id=north, device_id_type=MESH,
        ),
        pltpu.make_async_remote_copy(
            to_east, from_west, halo_send.at[2], halo_recv.at[2], device_id=east, device_id_type=MESH
        ),
        pltpu.make_async_remote_copy(
            to_west, from_east, halo_send.at[3], halo_recv.at[3], device_id=west, device_id_type=MESH
        ),
    ]
    for halo in halos:
        halo.start()

    def rows_arrive():
        pltpu.make_async_copy(edge(0), edge(0), halo_recv.at[0]).wait()
        pltpu.make_async_copy(edge(ROWS + 1), edge(ROWS + 1), halo_recv.at[1]).wait()

        @pl.when(lat == 0)
        def _():
            at = pl.ds(TILES, TILES)
            cells[at, :] = -cells[at, :]

        @pl.when(lat == N_LAT - 1)
        def _():
            at = pl.ds((ROWS + 1) * SLOT + TILES, TILES)
            cells[at, :] = -cells[at, :]

    late = (0, 2, PAIRS - 3, PAIRS - 1)

    def is_early(pair):
        ready = pair != late[0]
        for other_pair in late[1:]:
            ready = jnp.logical_and(ready, pair != other_pair)
        return ready

    @pl.when(polar)
    def _():
        def early(i, carry):
            near = partner(i)

            @pl.when(jnp.logical_and(near != lon, is_early(pair_of(near))))
            def _():
                go(pair_of(near), (lat, near)).start()

            @pl.when(near < AWAY)
            def _():
                go(pair_of(OWN + near), (other, near)).start()

            return carry

        lax.fori_loop(0, FAR, early, 0)
        rows_arrive()
        for j in (0, ROWS - 1):
            tendency(j, tend, False)
        value = corner()
        for j in (0, ROWS - 1):
            at = pl.ds(3 * j * TILES + FULL, 1)
            tend[at, :] = jnp.where(lane[:1] < TAIL, tend[at, :], value[j : j + 1])
        for target in (2, 3, N_LON - 2, N_LON - 1):

            @pl.when(lon != target)
            def _():
                go(pair_of(target), (lat, target)).start()

        lax.fori_loop(FAR, N_LON, early, 0)

    @pl.when(polar)
    def _():
        at = pl.ds(pl.multiple_of(place(lon) * TILES, 8), BLOCK)
        gathered[at, :] = tend[pl.ds(pl.multiple_of(pair_of(lon) * TILES, 8), BLOCK), :]

    def complete(pair, lat_row):
        inverse = geo[lat_row * 4]
        first_at, last_at = pl.ds(0, N_LON, stride=TILES), pl.ds(FULL, N_LON, stride=TILES)
        first, last = gathered[first_at, :], gathered[last_at, :]
        spot = lax.broadcasted_iota(jnp.int32, (N_LON, LANES), 1)
        half = N_LON // 2
        after = jnp.concatenate([last[half:], pltpu.roll(last[:half], half - 1, 0)], axis=0)
        before = jnp.concatenate([pltpu.roll(last[half:], 1, 0), last[:half]], axis=0)

        def pick(value, part, to):
            return pltpu.roll(value, (LANES + to - TAIL - part * LEVELS) % LANES, 1)

        end = TAIL - LEVELS
        h_first, h_end, u_first, u_end = 0, 1, 2, 3
        field = pair % 3

        def put(east, west):
            gathered[last_at, :] = jnp.where(spot < end, last, jnp.where(spot < TAIL, last + east, 0.0))
            gathered[first_at, :] = jnp.where(spot < LEVELS, first + west, first)

        @pl.when(field == 0)
        def _():
            h, u = pick(last, h_end, end), pick(last, u_end, end)
            east = (u + pick(after, u_first, end)) * (h + pick(after, h_first, end)) - u * h
            h, u = pick(last, h_first, 0), pick(last, u_first, 0)
            west = (u + pick(before, u_end, 0)) * (h + pick(before, h_end, 0)) - u * h
            put(-0.25 * inverse * east, 0.25 * inverse * west)

        @pl.when(field == 1)
        def _():
            put(-0.5 * inverse * pick(after, h_first, end), 0.5 * inverse * pick(before, h_end, 0))

    def circle(pair, first_row):
        lat_row = first_row + pair // 3
        complete(pair, lat_row)
        cutoff = cut[lat_row]
        data = jnp.concatenate([gathered[pl.ds(0, SIDE), :], gathered[pl.ds(SIDE, SIDE), :]], axis=1)
        lines = table_left(fore, 2 * FREQ, data)
        real, imag = lines[:FREQ], lines[FREQ:]
        cosine, sine = twiddle[pl.ds(0, FREQ), :], twiddle[pl.ds(FREQ, FREQ), :]
        turned = jnp.concatenate([real * cosine + imag * sine, imag * cosine - real * sine], axis=1)
        spectrum = table_right(turned, mix, 4 * LANES)
        wave = lax.broadcasted_iota(jnp.int32, (FREQ, 2 * LANES), 0) + BASE * (
            lax.broadcasted_iota(jnp.int32, (FREQ, 2 * LANES), 1) % LANES // LEVELS
        )
        wave = jnp.minimum(wave, NLON - wave)
        spectrum = jnp.where(wave <= cutoff, spectrum, 0.0)
        lines = table_right(spectrum, unmix, 2 * LANES)
        real, imag = lines[:, : 2 * LANES], lines[:, 2 * LANES :]
        turned = jnp.concatenate([real * cosine - imag * sine, real * sine + imag * cosine], axis=0)
        result = table_left(back, SIDE, turned)
        sent_back[pl.ds(0, SIDE), :] = result[:, :LANES]
        sent_back[pl.ds(SIDE, SIDE), :] = result[:, LANES:]

    def home(pair, sector, device):
        return pltpu.make_async_remote_copy(
            block(sent_back, place(sector)), block(returned, pair), back_send, back_recv,
            device_id=device, device_id_type=MESH,
        )

    def total(ref, blocks):
        return ref.at[pl.ds(0, blocks * BLOCK), :]

    def wait_for(ref, blocks, sem):
        pltpu.make_async_copy(total(ref, blocks), total(ref, blocks), sem).wait()

    @pl.when(lends)
    def _():
        for load in tables:
            load.wait()
        wait_for(gathered, N_LON, go_recv)
        circle(pair_of(OWN + lon), other * ROWS)

        def away(i, carry):
            target = partner(i)
            home(pair_of(OWN + lon), target, (other, target)).start()
            return carry

        lax.fori_loop(0, N_LON, away, 0)

    @pl.when(jnp.logical_not(polar))
    def _():
        rows_arrive()

    pltpu.make_async_copy(from_west, from_west, halo_recv.at[2]).wait()
    pltpu.make_async_copy(from_east, from_east, halo_recv.at[3]).wait()
    halos[0].wait_send()
    halos[1].wait_send()
    for i, f in enumerate(sides):
        at = pl.ds(SLOT + f * TILES + FULL, ROWS, stride=SLOT)
        here = from_east[pl.ds(i * ROWS, ROWS), :]
        cells[at, :] = jnp.where((lane >= TAIL) & (lane < TAIL + LEVELS), here, cells[at, :])
        at = pl.ds(SLOT + f * TILES + FULL + 1, ROWS, stride=SLOT)
        here = from_west[pl.ds(i * ROWS, ROWS), :]
        cells[at, :] = jnp.where(lane >= LANES - LEVELS, here, 0.0)

    @pl.when(jnp.logical_not(polar))
    def _():
        lax.fori_loop(0, ROWS, lambda j, c: (tendency(j, returned, True), c)[1], 0)

    def tracer(j, carry):
        inverse, sine, cos_north, cos_south = scalars(j)
        h, u, v, h_e, h_w, h_n, h_s, flux_e, flux_w, flux_n, flux_s = fluxes(j, cos_north, cos_south)
        for c in range(3):
            q, q_n, q_s = row(j + 1, 3 + c), row(j + 2, 3 + c), row(j, 3 + c)
            q_e, q_w = eastward(q), westward(q)
            zonal = flux_e * (0.5 * (q + q_e)) - flux_w * (0.5 * (q_w + q))
            merid = flux_n * (0.5 * (q + q_n)) - flux_s * (0.5 * (q_s + q))
            flux = (zonal + RATIO * merid) * inverse
            laplace = (q_e + q_w) + (q_n + q_s) - 4.0 * q
            at = pl.ds(pl.multiple_of((j * 3 + c) * TILES, 8), TILES)
            mass[at, :] = h * q + TIME_STEP * (DIFFUSION * laplace - flux)
        return carry

    lax.fori_loop(0, ROWS, tracer, 0)

    @pl.when(jnp.logical_not(lends))
    def _():
        for load in tables:
            load.wait()

    @pl.when(polar)
    def _():
        wait_for(gathered, N_LON - 1, go_recv)
        circle(pair_of(lon), lat * ROWS)

        def own(i, carry):
            target = partner(i)

            @pl.when(target != lon)
            def _():
                home(pair_of(lon), target, (lat, target)).start()

            return carry

        lax.fori_loop(0, N_LON, own, 0)
        at = pl.ds(pl.multiple_of(place(lon) * TILES, 8), BLOCK)
        returned[pl.ds(pl.multiple_of(pair_of(lon) * TILES, 8), BLOCK), :] = sent_back[at, :]

    halos[2].wait_send()
    halos[3].wait_send()

    @pl.when(polar)
    def _():
        wait_for(tend, PAIRS - 1, go_send)
        wait_for(sent_back, N_LON - 1, back_send)
        wait_for(returned, PAIRS - 1, back_recv)

    @pl.when(lends)
    def _():
        wait_for(sent_back, N_LON, back_send)


def finish(winds, thick, steps, mass, winds_out, thick_out, mass_out):
    def one_row(j, carry):
        start = j * 3 * TILES
        for t in range(FULL + 1):
            width = LANES if t < FULL else TAIL
            at = pl.ds(t * LANES, width)
            step = steps[pl.ds(start + TILES + t, 2, stride=TILES), :]
            winds_out[j, :, at] = winds[j, :, at] + TIME_STEP * step[:, :width]
            mass_out[j, :, at] = mass[pl.ds(start + t, 3, stride=TILES), :][:, :width].astype(BF16)
        return carry

    lax.fori_loop(0, ROWS, one_row, 0)
    for t in range(FULL + 1):
        width = LANES if t < FULL else TAIL
        at = pl.ds(t * LANES, width)
        thick_out[:, at] = thick[:, at] + TIME_STEP * steps[pl.ds(t, ROWS, stride=3 * TILES), :][:, :width]


def local(winds, thickness, tracers, cutoff):
    fore, twiddle, mix, unmix, back = filter_tables()
    anywhere = pl.BlockSpec(memory_space=pl.ANY)
    whole = pl.BlockSpec(memory_space=pltpu.VMEM)
    side = pltpu.VMEM((48, LANES), F32)
    dma = pltpu.SemaphoreType.DMA
    rows = jax.ShapeDtypeStruct((PAIRS * TILES, LANES), F32)
    winds = jnp.transpose(winds, (1, 0, 2))
    tracers = jnp.transpose(tracers, (1, 0, 2))
    steps, mass = pl.pallas_call(
        kernel,
        out_shape=(rows, rows),
        in_specs=[anywhere] * 10,
        out_specs=(whole, whole),
        scratch_shapes=[
            pltpu.VMEM((ROWS, 2, WIDE), F32),
            pltpu.VMEM((ROWS, WIDE), F32),
            pltpu.VMEM((ROWS, 3, WIDE), BF16),
            pltpu.VMEM(((ROWS + 2) * SLOT, LANES), F32),
            side, side, side, side,
            pltpu.VMEM((PAIRS * TILES, LANES), F32),
            pltpu.VMEM((N_LON * TILES, LANES), F32),
            pltpu.VMEM((N_LON * TILES, LANES), F32),
            pltpu.VMEM(fore.shape, BF16),
            pltpu.VMEM(twiddle.shape, F32),
            pltpu.VMEM(mix.shape, BF16),
            pltpu.VMEM(unmix.shape, BF16),
            pltpu.VMEM(back.shape, BF16),
            pltpu.SMEM((NLAT,), jnp.int32),
            pltpu.SMEM((4 * NLAT,), F32),
            dma((5,)), dma((5,)), dma((4,)), dma((4,)), dma, dma, dma, dma,
        ],
        compiler_params=pltpu.CompilerParams(
            collective_id=0, has_side_effects=True, vmem_limit_bytes=VMEM_MIB * 1024 * 1024
        ),
        name="substep",
    )(cutoff, geometry(), winds, thickness, tracers, fore, twiddle, mix, unmix, back)
    new_winds, new_thickness, new_mass = pl.pallas_call(
        finish,
        out_shape=(
            jax.ShapeDtypeStruct((ROWS, 2, WIDE), F32),
            jax.ShapeDtypeStruct((ROWS, WIDE), F32),
            jax.ShapeDtypeStruct((ROWS, 3, WIDE), BF16),
        ),
        in_specs=[whole] * 4,
        out_specs=(whole,) * 3,
        name="finish",
    )(winds, thickness, steps, mass)
    return jnp.transpose(new_winds, (1, 0, 2)), new_thickness, jnp.transpose(new_mass, (1, 0, 2))


def solution(mesh):
    in_specs = (P(None, "lat", "lon"), P("lat", "lon"), P(None, "lat", "lon"), P())
    out_specs = (P(None, "lat", "lon"), P("lat", "lon"), P(None, "lat", "lon"))
    return jax.shard_map(local, mesh=mesh, in_specs=in_specs, out_specs=out_specs, check_vma=False)
```

```python
import functools
import math

import jax
import jax.numpy as jnp
import numpy as np
from jax import lax
from jax.experimental import pallas as pl
from jax.experimental.pallas import tpu as pltpu
from jax.sharding import PartitionSpec as P

MESH = pl.DeviceIdType.MESH
F32 = jnp.float32
BF16 = jnp.bfloat16

LEVELS = 16
NLAT = 288
NLON = 2880
POLAR = 48
TIME_STEP = 0.05
DIFFUSION = 0.5
RATIO = 2.0 * NLAT / NLON

N_LAT = 32
N_LON = 16
ROWS = NLAT // N_LAT
COLS = NLON // N_LON
WIDE = COLS * LEVELS

LANES = 128
PER = LANES // LEVELS
TILES = 24
FULL = WIDE // LANES
TAIL = WIDE - FULL * LANES
FIELDS = 6
SLOT = FIELDS * TILES
EDGE = 5 * TILES
PAIRS = 3 * ROWS
BLOCK = FULL + 1
OWN = N_LON
FAR = 12
AWAY = PAIRS - OWN

BASE = NLON // PER
HALF = BASE // 2 + 1
FREQ = 184
VMEM_MIB = 63
SIDE = N_LON // 2 * TILES


def geometry():
    row = np.arange(NLAT, dtype=np.float64)
    centre = (row + 0.5) * (math.pi / NLAT) - math.pi / 2

    def face(index):
        inside = (index >= 0) & (index < NLAT - 1)
        return np.where(inside, np.sin((index + 1) * (math.pi / NLAT)), 0.0)

    table = np.stack([1.0 / np.cos(centre), np.sin(centre), face(row), face(row - 1)], axis=1)
    return table.astype(np.float32).reshape(-1)


def split_table(table):
    high = table.astype(np.float32).astype(jnp.bfloat16)
    low = (table - high.astype(np.float64)).astype(np.float32).astype(jnp.bfloat16)
    return np.concatenate([high, low], axis=0)


def filter_tables():
    turn = 2.0 * math.pi
    freq = np.arange(FREQ)
    live = (freq < HALF).astype(np.float64)
    sector, tile = (a.reshape(-1) for a in np.meshgrid(np.arange(N_LON // 2), np.arange(TILES), indexing="ij"))
    used = (tile * PER < COLS).astype(np.float64)
    place = 2 * COLS * sector // PER + tile
    angle = turn * ((freq[:, None] * place[None, :]) % BASE) / BASE
    weight = live[:, None] * used[None, :]
    fore = np.concatenate([np.cos(angle) * weight, -np.sin(angle) * weight], axis=0)
    twice = np.where((freq == 0) | (freq == HALF - 1), 1.0, 2.0) / NLON
    back = np.concatenate([np.cos(angle) * weight * twice[:, None], -np.sin(angle) * weight * twice[:, None]], axis=0).T

    lane = np.arange(2 * LANES)
    shift = lane % LANES // LEVELS + COLS * (lane // LANES)
    angle = turn * ((freq[:, None] * shift[None, :]) % NLON) / NLON
    twiddle = np.concatenate([np.cos(angle), np.sin(angle)], axis=0).astype(np.float32)

    out = np.arange(LANES)
    angle = turn * ((BASE * shift[:, None] * (out // LEVELS)[None, :]) % NLON) / NLON
    same = (lane % LEVELS)[:, None] == (out % LEVELS)[None, :]
    cosine, sine = np.cos(angle) * same, np.sin(angle) * same
    mix = np.concatenate(
        [np.concatenate([cosine, -sine], axis=1), np.concatenate([sine, cosine], axis=1)], axis=0
    )
    return split_table(fore), twiddle, split_table(mix), split_table(mix.T), split_table(back)


def split(value):
    high = value.astype(BF16)
    low = (value - high.astype(F32)).astype(BF16)
    return high, low


def dot(a, b):
    return jnp.dot(a, b, preferred_element_type=F32)


def table_left(table, rows, value):
    high, low = split(value)
    first = table[pl.ds(0, rows), :]
    return dot(first, high) + dot(first, low) + dot(table[pl.ds(rows, rows), :], high)


def table_right(value, table, rows):
    high, low = split(value)
    first = table[pl.ds(0, rows), :]
    return dot(high, first) + dot(low, first) + dot(high, table[pl.ds(rows, rows), :])


def eastward(value):
    lane = lax.broadcasted_iota(jnp.int32, (TILES, LANES), 1)
    here = pltpu.roll(value, LANES - LEVELS, 1)
    return jnp.where(lane < LANES - LEVELS, here, pltpu.roll(here, TILES - 1, 0))


def westward(value):
    lane = lax.broadcasted_iota(jnp.int32, (TILES, LANES), 1)
    here = pltpu.roll(value, LEVELS, 1)
    return jnp.where(lane >= LEVELS, here, pltpu.roll(here, 1, 0))


def kernel(
    cut_in, geo_in, winds_in, thick_in, mass_in, fore_in, twiddle_in, mix_in, unmix_in, back_in,
    returned, mass_out,
    wv, hv, qv, mv, mass, cells, to_east, to_west, from_west, from_east, tend, gathered, sent_back,
    fore, twiddle, mix, unmix, back, cut, geo,
    in_sem, table_sem, mass_sem, halo_send, halo_recv, go_send, go_recv, back_send, back_recv,
):
    lat = lax.axis_index("lat")
    lon = lax.axis_index("lon")
    polar_south = lat * ROWS < POLAR
    polar_north = (lat + 1) * ROWS > NLAT - POLAR
    polar = jnp.logical_or(polar_south, polar_north)
    other = (lat + N_LAT // 2) % N_LAT
    other_polar = jnp.logical_or(other * ROWS < POLAR, (other + 1) * ROWS > NLAT - POLAR)
    ring = N_LON // 2

    def away_place(sector):
        return (sector % ring + 2) % ring * 2 + sector // ring

    def partner(i):
        k = ring - 1 - i // 2
        offset = (k + 1) // 2 * (2 * (k % 2) - 1)
        return (lon // ring + i % 2) % 2 * ring + (lon % ring + offset + ring) % ring

    lends = jnp.logical_and(other_polar, away_place(lon) < AWAY)

    east = (lat, (lon + 1) % N_LON)
    west = (lat, (lon + N_LON - 1) % N_LON)
    below = (lat + N_LAT - 1) // N_LAT
    above = 1 - lat // (N_LAT - 1)
    south = (lat - below, (lon + (1 - below) * (N_LON // 2)) % N_LON)
    north = (lat + above, (lon + (1 - above) * (N_LON // 2)) % N_LON)

    barrier = pltpu.get_barrier_semaphore()

    def greet(device):
        pl.semaphore_signal(barrier, inc=1, device_id=device, device_id_type=MESH)

    @pl.when(polar)
    def _():
        def meet(i, carry):
            near = partner(i)

            @pl.when(away_place(near) < AWAY)
            def _():
                greet((other, near))

            @pl.when(near != lon)
            def _():
                greet((lat, near))

            return carry

        lax.fori_loop(0, N_LON, meet, 0)

    @pl.when(lends)
    def _():
        lax.fori_loop(0, N_LON, lambda i, c: (greet((other, partner(i))), c)[1], 0)

    for device in (south, north, east, west):
        greet(device)

    loads = [
        pltpu.make_async_copy(winds_in, wv, in_sem.at[0]),
        pltpu.make_async_copy(thick_in, hv, in_sem.at[1]),
        pltpu.make_async_copy(mass_in, qv, in_sem.at[2]),
        pltpu.make_async_copy(geo_in, geo, in_sem.at[3]),
        pltpu.make_async_copy(cut_in, cut, in_sem.at[4]),
    ]
    for load in loads:
        load.start()
    for load in loads:
        load.wait()
    tables = [
        pltpu.make_async_copy(source, target, table_sem.at[i])
        for i, (source, target) in enumerate(
            ((fore_in, fore), (twiddle_in, twiddle), (mix_in, mix), (unmix_in, unmix), (back_in, back))
        )
    ]
    for load in tables:
        load.start()

    def padded(value):
        return jnp.concatenate([value, jnp.zeros((value.shape[0], LANES - TAIL), F32)], axis=1)

    def place_row(j, carry):
        start = (j + 1) * SLOT
        for t in range(FULL + 1):
            at = pl.ds(t * LANES, LANES if t < FULL else TAIL)
            wind, ratio = wv[j, :, at], qv[j, :, at].astype(F32)
            if t == FULL:
                wind, ratio = padded(wind), padded(ratio)
            cells[pl.ds(start + t, 2, stride=TILES), :] = wind
            cells[pl.ds(start + 3 * TILES + t, 3, stride=TILES), :] = ratio
        cells[pl.ds(start + FULL + 1, FIELDS, stride=TILES), :] = jnp.zeros((FIELDS, LANES), F32)
        return carry

    lax.fori_loop(0, ROWS, place_row, 0)
    for t in range(FULL + 1):
        value = hv[:, pl.ds(t * LANES, LANES if t < FULL else TAIL)]
        cells[pl.ds(SLOT + 2 * TILES + t, ROWS, stride=SLOT), :] = value if t < FULL else padded(value)

    sides = (0, 2, 3, 4, 5)
    for i, f in enumerate(sides):
        first = cells[pl.ds(SLOT + f * TILES, ROWS, stride=SLOT), :]
        last = cells[pl.ds(SLOT + f * TILES + FULL, ROWS, stride=SLOT), :]
        to_west[pl.ds(i * ROWS, ROWS), :] = pltpu.roll(first, TAIL, 1)
        to_east[pl.ds(i * ROWS, ROWS), :] = pltpu.roll(last, LANES - TAIL, 1)

    gathered[pl.ds(FULL + 1, N_LON, stride=TILES), :] = jnp.zeros((N_LON, LANES), F32)

    def row(slot, field):
        return cells[pl.ds(pl.multiple_of(slot * SLOT + field * TILES, 8), TILES), :]

    def scalars(j):
        at = (lat * ROWS + j) * 4
        return geo[at], geo[at + 1], geo[at + 2], geo[at + 3]

    flat = lax.broadcasted_iota(jnp.int32, (TILES, LANES), 0) * LANES + lax.broadcasted_iota(
        jnp.int32, (TILES, LANES), 1
    )
    valid = flat < WIDE

    def fluxes(j, cos_north, cos_south):
        h, h_n, h_s = row(j + 1, 2), row(j + 2, 2), row(j, 2)
        v, v_n, v_s = row(j + 1, 1), row(j + 2, 1), row(j, 1)
        u = row(j + 1, 0)
        h_e, h_w = eastward(h), westward(h)
        flux_e = 0.5 * (u + eastward(u)) * (0.5 * (h + h_e))
        flux_w = 0.5 * (westward(u) + u) * (0.5 * (h_w + h))
        flux_n = 0.5 * (v + v_n) * (0.5 * (h + h_n)) * cos_north
        flux_s = 0.5 * (v_s + v) * (0.5 * (h_s + h)) * cos_south
        return h, u, v, h_e, h_w, h_n, h_s, flux_e, flux_w, flux_n, flux_s

    lane = lax.broadcasted_iota(jnp.int32, (ROWS, LANES), 1)

    def keep_row(j, f, target, value):
        at = pl.ds(pl.multiple_of((j * 3 + f) * TILES, 8), TILES)
        target[at, :] = jnp.where(valid, value, 0.0)

    def along(j):
        inverse, sine = scalars(j)[:2]
        h, v = row(j + 1, 2), row(j + 1, 1)
        return sine * v - (eastward(h) - westward(h)) * (0.5 * inverse)

    def tendency(j, target, both):
        inverse, sine, cos_north, cos_south = scalars(j)
        h, u, v, h_e, h_w, h_n, h_s, flux_e, flux_w, flux_n, flux_s = fluxes(j, cos_north, cos_south)
        keep_row(j, 0, target, -((flux_e - flux_w) + RATIO * (flux_n - flux_s)) * inverse)
        if both:
            keep_row(j, 1, target, sine * v - (h_e - h_w) * (0.5 * inverse))
        keep_row(j, 2, target, -sine * u - RATIO * (h_n - h_s) * 0.5)

    def corner():
        def column(field, tile, lanes):
            value = cells[pl.ds(SLOT + field * TILES + tile, ROWS, stride=SLOT), :]
            return pltpu.roll(value, lanes, 1)

        last = TAIL - LEVELS
        value = jnp.where(lane < TAIL + LEVELS, column(2, 0, TAIL), column(2, FULL, TAIL + LEVELS - last))
        value = jnp.where(lane < TAIL + 2 * LEVELS, value, column(0, 0, TAIL + 2 * LEVELS))
        return jnp.where(lane < TAIL + 3 * LEVELS, value, column(0, FULL, TAIL + 3 * LEVELS - last))

    @pl.when(polar)
    def _():
        lax.fori_loop(1, ROWS - 1, lambda j, c: (tendency(j, tend, True), c)[1], 0)
        for j in (0, ROWS - 1):
            keep_row(j, 1, tend, along(j))
        value = corner()
        at = pl.ds(TILES + FULL, ROWS, stride=3 * TILES)
        tend[at, :] = jnp.where(lane < TAIL, tend[at, :], value)
        at = pl.ds(3 * TILES + FULL, ROWS - 2, stride=3 * TILES)
        inner = slice(1, ROWS - 1)
        tend[at, :] = jnp.where(lane[inner] < TAIL, tend[at, :], value[inner])

    def pair_of(i):
        return (2 * i + PAIRS - 4) % PAIRS

    def block(ref, index):
        return ref.at[pl.ds(pl.multiple_of(index * TILES, 8), BLOCK), :]

    def place(sector):
        return (sector % 2) * (N_LON // 2) + sector // 2

    def go(pair, device):
        return pltpu.make_async_remote_copy(
            block(tend, pair), block(gathered, place(lon)), go_send, go_recv, device_id=device, device_id_type=MESH
        )

    @pl.when(polar)
    def _():
        pl.semaphore_wait(barrier, 4 + N_LON - 1 + AWAY)

    @pl.when(lends)
    def _():
        pl.semaphore_wait(barrier, 4 + N_LON)

    @pl.when(jnp.logical_not(jnp.logical_or(polar, lends)))
    def _():
        pl.semaphore_wait(barrier, 4)

    south_slot = below * (ROWS + 1)
    north_slot = (1 - above) * (ROWS + 1)

    def edge(slot):
        return cells.at[pl.ds(pl.multiple_of(slot * SLOT + TILES, 8), EDGE), :]

    halos = [
        pltpu.make_async_remote_copy(
            edge(1), edge(south_slot), halo_send.at[0], halo_recv.at[below], device_id=south, device_id_type=MESH
        ),
        pltpu.make_async_remote_copy(
            edge(ROWS), edge(north_slot), halo_send.at[1], halo_recv.at[1 - above],
            device_id=north, device_id_type=MESH,
        ),
        pltpu.make_async_remote_copy(
            to_east, from_west, halo_send.at[2], halo_recv.at[2], device_id=east, device_id_type=MESH
        ),
        pltpu.make_async_remote_copy(
            to_west, from_east, halo_send.at[3], halo_recv.at[3], device_id=west, device_id_type=MESH
        ),
    ]
    for halo in halos:
        halo.start()

    def rows_arrive():
        pltpu.make_async_copy(edge(0), edge(0), halo_recv.at[0]).wait()
        pltpu.make_async_copy(edge(ROWS + 1), edge(ROWS + 1), halo_recv.at[1]).wait()

        @pl.when(lat == 0)
        def _():
            at = pl.ds(TILES, TILES)
            cells[at, :] = -cells[at, :]

        @pl.when(lat == N_LAT - 1)
        def _():
            at = pl.ds((ROWS + 1) * SLOT + TILES, TILES)
            cells[at, :] = -cells[at, :]

    late = (0, 2, PAIRS - 3, PAIRS - 1)

    def is_early(pair):
        ready = pair != late[0]
        for other_pair in late[1:]:
            ready = jnp.logical_and(ready, pair != other_pair)
        return ready

    @pl.when(polar)
    def _():
        def early(i, carry):
            near = partner(i)

            @pl.when(jnp.logical_and(near != lon, is_early(pair_of(near))))
            def _():
                go(pair_of(near), (lat, near)).start()

            @pl.when(away_place(near) < AWAY)
            def _():
                go(pair_of(OWN + away_place(near)), (other, near)).start()

            return carry

        lax.fori_loop(0, FAR, early, 0)
        rows_arrive()
        for j in (0, ROWS - 1):
            tendency(j, tend, False)
        value = corner()
        for j in (0, ROWS - 1):
            at = pl.ds(3 * j * TILES + FULL, 1)
            tend[at, :] = jnp.where(lane[:1] < TAIL, tend[at, :], value[j : j + 1])
        for target in (2, 3, N_LON - 2, N_LON - 1):

            @pl.when(lon != target)
            def _():
                go(pair_of(target), (lat, target)).start()

        lax.fori_loop(FAR, N_LON, early, 0)

    @pl.when(polar)
    def _():
        at = pl.ds(pl.multiple_of(place(lon) * TILES, 8), BLOCK)
        gathered[at, :] = tend[pl.ds(pl.multiple_of(pair_of(lon) * TILES, 8), BLOCK), :]

    def complete(pair, lat_row):
        inverse = geo[lat_row * 4]
        first_at, last_at = pl.ds(0, N_LON, stride=TILES), pl.ds(FULL, N_LON, stride=TILES)
        first, last = gathered[first_at, :], gathered[last_at, :]
        spot = lax.broadcasted_iota(jnp.int32, (N_LON, LANES), 1)
        half = N_LON // 2
        after = jnp.concatenate([last[half:], pltpu.roll(last[:half], half - 1, 0)], axis=0)
        before = jnp.concatenate([pltpu.roll(last[half:], 1, 0), last[:half]], axis=0)

        def pick(value, part, to):
            return pltpu.roll(value, (LANES + to - TAIL - part * LEVELS) % LANES, 1)

        end = TAIL - LEVELS
        h_first, h_end, u_first, u_end = 0, 1, 2, 3
        field = pair % 3

        def put(east, west):
            gathered[last_at, :] = jnp.where(spot < end, last, jnp.where(spot < TAIL, last + east, 0.0))
            gathered[first_at, :] = jnp.where(spot < LEVELS, first + west, first)

        @pl.when(field == 0)
        def _():
            h, u = pick(last, h_end, end), pick(last, u_end, end)
            east = (u + pick(after, u_first, end)) * (h + pick(after, h_first, end)) - u * h
            h, u = pick(last, h_first, 0), pick(last, u_first, 0)
            west = (u + pick(before, u_end, 0)) * (h + pick(before, h_end, 0)) - u * h
            put(-0.25 * inverse * east, 0.25 * inverse * west)

        @pl.when(field == 1)
        def _():
            put(-0.5 * inverse * pick(after, h_first, end), 0.5 * inverse * pick(before, h_end, 0))

    def circle(pair, first_row):
        lat_row = first_row + pair // 3
        complete(pair, lat_row)
        cutoff = cut[lat_row]
        data = jnp.concatenate([gathered[pl.ds(0, SIDE), :], gathered[pl.ds(SIDE, SIDE), :]], axis=1)
        lines = table_left(fore, 2 * FREQ, data)
        real, imag = lines[:FREQ], lines[FREQ:]
        cosine, sine = twiddle[pl.ds(0, FREQ), :], twiddle[pl.ds(FREQ, FREQ), :]
        turned = jnp.concatenate([real * cosine + imag * sine, imag * cosine - real * sine], axis=1)
        spectrum = table_right(turned, mix, 4 * LANES)
        wave = lax.broadcasted_iota(jnp.int32, (FREQ, 2 * LANES), 0) + BASE * (
            lax.broadcasted_iota(jnp.int32, (FREQ, 2 * LANES), 1) % LANES // LEVELS
        )
        wave = jnp.minimum(wave, NLON - wave)
        spectrum = jnp.where(wave <= cutoff, spectrum, 0.0)
        lines = table_right(spectrum, unmix, 2 * LANES)
        real, imag = lines[:, : 2 * LANES], lines[:, 2 * LANES :]
        turned = jnp.concatenate([real * cosine - imag * sine, real * sine + imag * cosine], axis=0)
        result = table_left(back, SIDE, turned)
        sent_back[pl.ds(0, SIDE), :] = result[:, :LANES]
        sent_back[pl.ds(SIDE, SIDE), :] = result[:, LANES:]

    def home(pair, sector, device):
        return pltpu.make_async_remote_copy(
            block(sent_back, place(sector)), block(returned, pair), back_send, back_recv,
            device_id=device, device_id_type=MESH,
        )

    def total(ref, blocks):
        return ref.at[pl.ds(0, blocks * BLOCK), :]

    def wait_for(ref, blocks, sem):
        pltpu.make_async_copy(total(ref, blocks), total(ref, blocks), sem).wait()

    @pl.when(lends)
    def _():
        for load in tables:
            load.wait()
        wait_for(gathered, N_LON, go_recv)
        circle(pair_of(OWN + away_place(lon)), other * ROWS)

        def away(i, carry):
            target = partner(i)
            home(pair_of(OWN + away_place(lon)), target, (other, target)).start()
            return carry

        lax.fori_loop(0, N_LON, away, 0)

    @pl.when(jnp.logical_not(polar))
    def _():
        rows_arrive()

    pltpu.make_async_copy(from_west, from_west, halo_recv.at[2]).wait()
    pltpu.make_async_copy(from_east, from_east, halo_recv.at[3]).wait()
    halos[0].wait_send()
    halos[1].wait_send()
    for i, f in enumerate(sides):
        at = pl.ds(SLOT + f * TILES + FULL, ROWS, stride=SLOT)
        here = from_east[pl.ds(i * ROWS, ROWS), :]
        cells[at, :] = jnp.where((lane >= TAIL) & (lane < TAIL + LEVELS), here, cells[at, :])
        at = pl.ds(SLOT + f * TILES + FULL + 1, ROWS, stride=SLOT)
        here = from_west[pl.ds(i * ROWS, ROWS), :]
        cells[at, :] = jnp.where(lane >= LANES - LEVELS, here, 0.0)

    @pl.when(jnp.logical_not(polar))
    def _():
        lax.fori_loop(0, ROWS, lambda j, c: (tendency(j, returned, True), c)[1], 0)

    def tracer(j, carry):
        inverse, sine, cos_north, cos_south = scalars(j)
        h, u, v, h_e, h_w, h_n, h_s, flux_e, flux_w, flux_n, flux_s = fluxes(j, cos_north, cos_south)
        for c in range(3):
            q, q_n, q_s = row(j + 1, 3 + c), row(j + 2, 3 + c), row(j, 3 + c)
            q_e, q_w = eastward(q), westward(q)
            zonal = flux_e * (0.5 * (q + q_e)) - flux_w * (0.5 * (q_w + q))
            merid = flux_n * (0.5 * (q + q_n)) - flux_s * (0.5 * (q_s + q))
            flux = (zonal + RATIO * merid) * inverse
            laplace = (q_e + q_w) + (q_n + q_s) - 4.0 * q
            at = pl.ds(pl.multiple_of((j * 3 + c) * TILES, 8), TILES)
            mass[at, :] = h * q + TIME_STEP * (DIFFUSION * laplace - flux)
        return carry

    lax.fori_loop(0, ROWS, tracer, 0)

    def narrow(j, carry):
        for t in range(FULL + 1):
            width = LANES if t < FULL else TAIL
            value = mass[pl.ds(j * 3 * TILES + t, 3, stride=TILES), :]
            mv[j, :, pl.ds(t * LANES, width)] = value[:, :width].astype(BF16)
        return carry

    lax.fori_loop(0, ROWS, narrow, 0)
    keep_mass = pltpu.make_async_copy(mv, mass_out, mass_sem)
    keep_mass.start()

    @pl.when(jnp.logical_not(lends))
    def _():
        for load in tables:
            load.wait()

    @pl.when(polar)
    def _():
        wait_for(gathered, N_LON - 1, go_recv)
        circle(pair_of(lon), lat * ROWS)

        def own(i, carry):
            target = partner(i)

            @pl.when(target != lon)
            def _():
                home(pair_of(lon), target, (lat, target)).start()

            return carry

        lax.fori_loop(0, N_LON, own, 0)
        at = pl.ds(pl.multiple_of(place(lon) * TILES, 8), BLOCK)
        returned[pl.ds(pl.multiple_of(pair_of(lon) * TILES, 8), BLOCK), :] = sent_back[at, :]

    halos[2].wait_send()
    halos[3].wait_send()
    keep_mass.wait()

    @pl.when(polar)
    def _():
        wait_for(tend, PAIRS - 1, go_send)
        wait_for(sent_back, N_LON - 1, back_send)
        wait_for(returned, PAIRS - 1, back_recv)

    @pl.when(lends)
    def _():
        wait_for(sent_back, N_LON, back_send)


def finish(winds, thick, steps, mass, winds_out, thick_out, mass_out, wv, hv, sv, mv, in_sem, out_sem):
    def pair(n, source, held, target):
        return pltpu.make_async_copy(source, held, in_sem.at[n]), pltpu.make_async_copy(held, target, out_sem.at[n])

    mass_load, mass_store = pair(0, mass, mv, mass_out)
    wind_load, wind_store = pair(1, winds, wv, winds_out)
    thick_load, thick_store = pair(2, thick, hv, thick_out)
    steps_load = pltpu.make_async_copy(steps, sv, in_sem.at[3])
    for load in (steps_load, wind_load, thick_load, mass_load):
        load.start()
    steps_load.wait()
    wind_load.wait()

    def one_row(j, carry):
        for t in range(FULL + 1):
            width = LANES if t < FULL else TAIL
            at = pl.ds(t * LANES, width)
            step = sv[pl.ds((j * 3 + 1) * TILES + t, 2, stride=TILES), :]
            wv[j, :, at] = wv[j, :, at] + TIME_STEP * step[:, :width]
        return carry

    lax.fori_loop(0, ROWS, one_row, 0)
    wind_store.start()
    mass_load.wait()
    mass_store.start()
    thick_load.wait()
    for t in range(FULL + 1):
        width = LANES if t < FULL else TAIL
        at = pl.ds(t * LANES, width)
        hv[:, at] = hv[:, at] + TIME_STEP * sv[pl.ds(t, ROWS, stride=3 * TILES), :][:, :width]
    thick_store.start()
    for store in (wind_store, mass_store, thick_store):
        store.wait()


def local(winds, thickness, tracers, cutoff):
    fore, twiddle, mix, unmix, back = filter_tables()
    anywhere = pl.BlockSpec(memory_space=pl.ANY)
    whole = pl.BlockSpec(memory_space=pltpu.VMEM)
    side = pltpu.VMEM((48, LANES), F32)
    dma = pltpu.SemaphoreType.DMA
    rows = jax.ShapeDtypeStruct((PAIRS * TILES, LANES), F32)
    winds = jnp.transpose(winds, (1, 0, 2))
    tracers = jnp.transpose(tracers, (1, 0, 2))
    steps, mass = pl.pallas_call(
        kernel,
        out_shape=(rows, jax.ShapeDtypeStruct((ROWS, 3, WIDE), BF16)),
        in_specs=[anywhere] * 10,
        out_specs=(whole, anywhere),
        scratch_shapes=[
            pltpu.VMEM((ROWS, 2, WIDE), F32),
            pltpu.VMEM((ROWS, WIDE), F32),
            pltpu.VMEM((ROWS, 3, WIDE), BF16),
            pltpu.VMEM((ROWS, 3, WIDE), BF16),
            pltpu.VMEM((PAIRS * TILES, LANES), F32),
            pltpu.VMEM(((ROWS + 2) * SLOT, LANES), F32),
            side, side, side, side,
            pltpu.VMEM((PAIRS * TILES, LANES), F32),
            pltpu.VMEM((N_LON * TILES, LANES), F32),
            pltpu.VMEM((N_LON * TILES, LANES), F32),
            pltpu.VMEM(fore.shape, BF16),
            pltpu.VMEM(twiddle.shape, F32),
            pltpu.VMEM(mix.shape, BF16),
            pltpu.VMEM(unmix.shape, BF16),
            pltpu.VMEM(back.shape, BF16),
            pltpu.SMEM((NLAT,), jnp.int32),
            pltpu.SMEM((4 * NLAT,), F32),
            dma((5,)), dma((5,)), dma, dma((4,)), dma((4,)), dma, dma, dma, dma,
        ],
        compiler_params=pltpu.CompilerParams(
            collective_id=0, has_side_effects=True, vmem_limit_bytes=VMEM_MIB * 1024 * 1024
        ),
        name="substep",
    )(cutoff, geometry(), winds, thickness, tracers, fore, twiddle, mix, unmix, back)
    new_winds, new_thickness, new_mass = pl.pallas_call(
        finish,
        out_shape=(
            jax.ShapeDtypeStruct((ROWS, 2, WIDE), F32),
            jax.ShapeDtypeStruct((ROWS, WIDE), F32),
            jax.ShapeDtypeStruct((ROWS, 3, WIDE), BF16),
        ),
        in_specs=[anywhere] * 4,
        out_specs=(anywhere,) * 3,
        scratch_shapes=[
            pltpu.VMEM((ROWS, 2, WIDE), F32),
            pltpu.VMEM((ROWS, WIDE), F32),
            pltpu.VMEM((PAIRS * TILES, LANES), F32),
            pltpu.VMEM((ROWS, 3, WIDE), BF16),
            dma((4,)), dma((3,)),
        ],
        compiler_params=pltpu.CompilerParams(vmem_limit_bytes=VMEM_MIB * 1024 * 1024),
        name="finish",
    )(winds, thickness, steps, mass)
    return jnp.transpose(new_winds, (1, 0, 2)), new_thickness, jnp.transpose(new_mass, (1, 0, 2))


def solution(mesh):
    in_specs = (P(None, "lat", "lon"), P("lat", "lon"), P(None, "lat", "lon"), P())
    out_specs = (P(None, "lat", "lon"), P("lat", "lon"), P(None, "lat", "lon"))
    return jax.shard_map(local, mesh=mesh, in_specs=in_specs, out_specs=out_specs, check_vma=False)
```

```python
import functools
import math

import jax
import jax.numpy as jnp
import numpy as np
from jax import lax
from jax.experimental import pallas as pl
from jax.experimental.pallas import tpu as pltpu
from jax.sharding import PartitionSpec as P

MESH = pl.DeviceIdType.MESH
F32 = jnp.float32
BF16 = jnp.bfloat16

LEVELS = 16
NLAT = 288
NLON = 2880
POLAR = 48
TIME_STEP = 0.05
DIFFUSION = 0.5
RATIO = 2.0 * NLAT / NLON

N_LAT = 32
N_LON = 16
ROWS = NLAT // N_LAT
COLS = NLON // N_LON
WIDE = COLS * LEVELS

LANES = 128
PER = LANES // LEVELS
TILES = 24
FULL = WIDE // LANES
TAIL = WIDE - FULL * LANES
FIELDS = 6
SLOT = FIELDS * TILES
EDGE = 5 * TILES
PAIRS = 3 * ROWS
BLOCK = FULL + 1
OWN = N_LON
FAR = 12
AWAY = PAIRS - OWN

BASE = NLON // PER
HALF = BASE // 2 + 1
FREQ = 184
VMEM_MIB = 63
SIDE = N_LON // 2 * TILES


def geometry():
    row = np.arange(NLAT, dtype=np.float64)
    centre = (row + 0.5) * (math.pi / NLAT) - math.pi / 2

    def face(index):
        inside = (index >= 0) & (index < NLAT - 1)
        return np.where(inside, np.sin((index + 1) * (math.pi / NLAT)), 0.0)

    table = np.stack([1.0 / np.cos(centre), np.sin(centre), face(row), face(row - 1)], axis=1)
    return table.astype(np.float32).reshape(-1)


def filter_tables():
    turn = 2.0 * math.pi
    freq = np.arange(FREQ)
    live = (freq < HALF).astype(np.float64)
    sector, tile = (a.reshape(-1) for a in np.meshgrid(np.arange(N_LON // 2), np.arange(TILES), indexing="ij"))
    used = (tile * PER < COLS).astype(np.float64)
    place = 2 * COLS * sector // PER + tile
    angle = turn * ((freq[:, None] * place[None, :]) % BASE) / BASE
    weight = live[:, None] * used[None, :]
    fore = np.concatenate([np.cos(angle) * weight, -np.sin(angle) * weight], axis=0)
    twice = np.where((freq == 0) | (freq == HALF - 1), 1.0, 2.0) / NLON
    back = np.concatenate([np.cos(angle) * weight * twice[:, None], -np.sin(angle) * weight * twice[:, None]], axis=0).T

    lane = np.arange(2 * LANES)
    shift = lane % LANES // LEVELS + COLS * (lane // LANES)
    angle = turn * ((freq[:, None] * shift[None, :]) % NLON) / NLON
    twiddle = np.concatenate([np.cos(angle), np.sin(angle)], axis=0).astype(np.float32)

    out = np.arange(LANES)
    angle = turn * ((BASE * shift[:, None] * (out // LEVELS)[None, :]) % NLON) / NLON
    same = (lane % LEVELS)[:, None] == (out % LEVELS)[None, :]
    cosine, sine = np.cos(angle) * same, np.sin(angle) * same
    mix = np.concatenate(
        [np.concatenate([cosine, -sine], axis=1), np.concatenate([sine, cosine], axis=1)], axis=0
    )
    fore, mix, unmix, back = (a.astype(np.float32).astype(jnp.bfloat16) for a in (fore, mix, mix.T, back))
    return fore, twiddle, mix, unmix, back


def dot(a, b):
    return jnp.dot(a.astype(BF16), b.astype(BF16), preferred_element_type=F32)


def eastward(value):
    lane = lax.broadcasted_iota(jnp.int32, (TILES, LANES), 1)
    here = pltpu.roll(value, LANES - LEVELS, 1)
    return jnp.where(lane < LANES - LEVELS, here, pltpu.roll(here, TILES - 1, 0))


def westward(value):
    lane = lax.broadcasted_iota(jnp.int32, (TILES, LANES), 1)
    here = pltpu.roll(value, LEVELS, 1)
    return jnp.where(lane >= LEVELS, here, pltpu.roll(here, 1, 0))


def kernel(
    cut_in, geo_in, winds_in, thick_in, mass_in, fore_in, twiddle_in, mix_in, unmix_in, back_in,
    returned, mass_out,
    wv, hv, qv, mv, mass, cells, to_east, to_west, from_west, from_east, tend, gathered, sent_back,
    fore, twiddle, mix, unmix, back, cut, geo,
    in_sem, table_sem, mass_sem, keep_sem, halo_send, halo_recv, go_send, go_recv, back_send, back_recv,
):
    lat = lax.axis_index("lat")
    lon = lax.axis_index("lon")
    polar_south = lat * ROWS < POLAR
    polar_north = (lat + 1) * ROWS > NLAT - POLAR
    polar = jnp.logical_or(polar_south, polar_north)
    other = (lat + N_LAT // 2) % N_LAT
    other_polar = jnp.logical_or(other * ROWS < POLAR, (other + 1) * ROWS > NLAT - POLAR)
    ring = N_LON // 2

    def away_place(sector):
        return (sector % ring + 2) % ring * 2 + sector // ring

    def partner(i):
        k = ring - 1 - i // 2
        offset = (k + 1) // 2 * (2 * (k % 2) - 1)
        return (lon // ring + i % 2) % 2 * ring + (lon % ring + offset + ring) % ring

    lends = jnp.logical_and(other_polar, away_place(lon) < AWAY)

    east = (lat, (lon + 1) % N_LON)
    west = (lat, (lon + N_LON - 1) % N_LON)
    below = (lat + N_LAT - 1) // N_LAT
    above = 1 - lat // (N_LAT - 1)
    south = (lat - below, (lon + (1 - below) * (N_LON // 2)) % N_LON)
    north = (lat + above, (lon + (1 - above) * (N_LON // 2)) % N_LON)

    barrier = pltpu.get_barrier_semaphore()

    def greet(device):
        pl.semaphore_signal(barrier, inc=1, device_id=device, device_id_type=MESH)

    @pl.when(polar)
    def _():
        def meet(i, carry):
            near = partner(i)

            @pl.when(away_place(near) < AWAY)
            def _():
                greet((other, near))

            @pl.when(near != lon)
            def _():
                greet((lat, near))

            return carry

        lax.fori_loop(0, N_LON, meet, 0)

    @pl.when(lends)
    def _():
        lax.fori_loop(0, N_LON, lambda i, c: (greet((other, partner(i))), c)[1], 0)

    for device in (south, north, east, west):
        greet(device)

    loads = [
        pltpu.make_async_copy(winds_in, wv, in_sem.at[0]),
        pltpu.make_async_copy(thick_in, hv, in_sem.at[1]),
        pltpu.make_async_copy(mass_in, qv, in_sem.at[2]),
        pltpu.make_async_copy(geo_in, geo, in_sem.at[3]),
        pltpu.make_async_copy(cut_in, cut, in_sem.at[4]),
    ]
    for load in loads:
        load.start()
    for load in loads:
        load.wait()
    tables = [
        pltpu.make_async_copy(source, target, table_sem.at[i])
        for i, (source, target) in enumerate(
            ((fore_in, fore), (twiddle_in, twiddle), (mix_in, mix), (unmix_in, unmix), (back_in, back))
        )
    ]
    for load in tables:
        load.start()

    def padded(value):
        return jnp.concatenate([value, jnp.zeros((value.shape[0], LANES - TAIL), F32)], axis=1)

    def place_row(j, carry):
        start = (j + 1) * SLOT
        for t in range(FULL + 1):
            at = pl.ds(t * LANES, LANES if t < FULL else TAIL)
            wind, ratio = wv[j, :, at], qv[j, :, at].astype(F32)
            if t == FULL:
                wind, ratio = padded(wind), padded(ratio)
            cells[pl.ds(start + t, 2, stride=TILES), :] = wind
            cells[pl.ds(start + 3 * TILES + t, 3, stride=TILES), :] = ratio
        cells[pl.ds(start + FULL + 1, FIELDS, stride=TILES), :] = jnp.zeros((FIELDS, LANES), F32)
        return carry

    lax.fori_loop(0, ROWS, place_row, 0)
    for t in range(FULL + 1):
        value = hv[:, pl.ds(t * LANES, LANES if t < FULL else TAIL)]
        cells[pl.ds(SLOT + 2 * TILES + t, ROWS, stride=SLOT), :] = value if t < FULL else padded(value)

    sides = (0, 2, 3, 4, 5)
    for i, f in enumerate(sides):
        first = cells[pl.ds(SLOT + f * TILES, ROWS, stride=SLOT), :]
        last = cells[pl.ds(SLOT + f * TILES + FULL, ROWS, stride=SLOT), :]
        to_west[pl.ds(i * ROWS, ROWS), :] = pltpu.roll(first, TAIL, 1)
        to_east[pl.ds(i * ROWS, ROWS), :] = pltpu.roll(last, LANES - TAIL, 1)

    gathered[pl.ds(FULL + 1, N_LON, stride=TILES), :] = jnp.zeros((N_LON, LANES), F32)

    def row(slot, field):
        return cells[pl.ds(pl.multiple_of(slot * SLOT + field * TILES, 8), TILES), :]

    def scalars(j):
        at = (lat * ROWS + j) * 4
        return geo[at], geo[at + 1], geo[at + 2], geo[at + 3]

    flat = lax.broadcasted_iota(jnp.int32, (TILES, LANES), 0) * LANES + lax.broadcasted_iota(
        jnp.int32, (TILES, LANES), 1
    )
    valid = flat < WIDE

    def fluxes(j, cos_north, cos_south):
        h, h_n, h_s = row(j + 1, 2), row(j + 2, 2), row(j, 2)
        v, v_n, v_s = row(j + 1, 1), row(j + 2, 1), row(j, 1)
        u = row(j + 1, 0)
        h_e, h_w = eastward(h), westward(h)
        flux_e = 0.5 * (u + eastward(u)) * (0.5 * (h + h_e))
        flux_w = 0.5 * (westward(u) + u) * (0.5 * (h_w + h))
        flux_n = 0.5 * (v + v_n) * (0.5 * (h + h_n)) * cos_north
        flux_s = 0.5 * (v_s + v) * (0.5 * (h_s + h)) * cos_south
        return h, u, v, h_e, h_w, h_n, h_s, flux_e, flux_w, flux_n, flux_s

    lane = lax.broadcasted_iota(jnp.int32, (ROWS, LANES), 1)

    def keep_row(j, f, target, value):
        at = pl.ds(pl.multiple_of((j * 3 + f) * TILES, 8), TILES)
        target[at, :] = jnp.where(valid, value, 0.0)

    def along(j):
        inverse, sine = scalars(j)[:2]
        h, v = row(j + 1, 2), row(j + 1, 1)
        return sine * v - (eastward(h) - westward(h)) * (0.5 * inverse)

    def tendency(j, target, both):
        inverse, sine, cos_north, cos_south = scalars(j)
        h, u, v, h_e, h_w, h_n, h_s, flux_e, flux_w, flux_n, flux_s = fluxes(j, cos_north, cos_south)
        keep_row(j, 0, target, -((flux_e - flux_w) + RATIO * (flux_n - flux_s)) * inverse)
        if both:
            keep_row(j, 1, target, sine * v - (h_e - h_w) * (0.5 * inverse))
        keep_row(j, 2, target, -sine * u - RATIO * (h_n - h_s) * 0.5)

    def corner():
        def column(field, tile, lanes):
            value = cells[pl.ds(SLOT + field * TILES + tile, ROWS, stride=SLOT), :]
            return pltpu.roll(value, lanes, 1)

        last = TAIL - LEVELS
        value = jnp.where(lane < TAIL + LEVELS, column(2, 0, TAIL), column(2, FULL, TAIL + LEVELS - last))
        value = jnp.where(lane < TAIL + 2 * LEVELS, value, column(0, 0, TAIL + 2 * LEVELS))
        return jnp.where(lane < TAIL + 3 * LEVELS, value, column(0, FULL, TAIL + 3 * LEVELS - last))

    @pl.when(polar)
    def _():
        lax.fori_loop(1, ROWS - 1, lambda j, c: (tendency(j, tend, True), c)[1], 0)
        for j in (0, ROWS - 1):
            keep_row(j, 1, tend, along(j))
        value = corner()
        at = pl.ds(TILES + FULL, ROWS, stride=3 * TILES)
        tend[at, :] = jnp.where(lane < TAIL, tend[at, :], value)
        at = pl.ds(3 * TILES + FULL, ROWS - 2, stride=3 * TILES)
        inner = slice(1, ROWS - 1)
        tend[at, :] = jnp.where(lane[inner] < TAIL, tend[at, :], value[inner])

    def pair_of(i):
        return (2 * i + PAIRS - 4) % PAIRS

    def block(ref, index):
        return ref.at[pl.ds(pl.multiple_of(index * TILES, 8), BLOCK), :]

    def place(sector):
        return (sector % 2) * (N_LON // 2) + sector // 2

    def go(pair, device):
        return pltpu.make_async_remote_copy(
            block(tend, pair), block(gathered, place(lon)), go_send, go_recv, device_id=device, device_id_type=MESH
        )

    @pl.when(polar)
    def _():
        pl.semaphore_wait(barrier, 4 + N_LON - 1 + AWAY)

    @pl.when(lends)
    def _():
        pl.semaphore_wait(barrier, 4 + N_LON)

    @pl.when(jnp.logical_not(jnp.logical_or(polar, lends)))
    def _():
        pl.semaphore_wait(barrier, 4)

    south_slot = below * (ROWS + 1)
    north_slot = (1 - above) * (ROWS + 1)

    def edge(slot):
        return cells.at[pl.ds(pl.multiple_of(slot * SLOT + TILES, 8), EDGE), :]

    halos = [
        pltpu.make_async_remote_copy(
            edge(1), edge(south_slot), halo_send.at[0], halo_recv.at[below], device_id=south, device_id_type=MESH
        ),
        pltpu.make_async_remote_copy(
            edge(ROWS), edge(north_slot), halo_send.at[1], halo_recv.at[1 - above],
            device_id=north, device_id_type=MESH,
        ),
        pltpu.make_async_remote_copy(
            to_east, from_west, halo_send.at[2], halo_recv.at[2], device_id=east, device_id_type=MESH
        ),
        pltpu.make_async_remote_copy(
            to_west, from_east, halo_send.at[3], halo_recv.at[3], device_id=west, device_id_type=MESH
        ),
    ]
    for halo in halos:
        halo.start()

    def rows_arrive():
        pltpu.make_async_copy(edge(0), edge(0), halo_recv.at[0]).wait()
        pltpu.make_async_copy(edge(ROWS + 1), edge(ROWS + 1), halo_recv.at[1]).wait()

        @pl.when(lat == 0)
        def _():
            at = pl.ds(TILES, TILES)
            cells[at, :] = -cells[at, :]

        @pl.when(lat == N_LAT - 1)
        def _():
            at = pl.ds((ROWS + 1) * SLOT + TILES, TILES)
            cells[at, :] = -cells[at, :]

    late = (0, 2, PAIRS - 3, PAIRS - 1)

    def is_early(pair):
        ready = pair != late[0]
        for other_pair in late[1:]:
            ready = jnp.logical_and(ready, pair != other_pair)
        return ready

    @pl.when(polar)
    def _():
        def early(i, carry):
            near = partner(i)

            @pl.when(jnp.logical_and(near != lon, is_early(pair_of(near))))
            def _():
                go(pair_of(near), (lat, near)).start()

            @pl.when(away_place(near) < AWAY)
            def _():
                go(pair_of(OWN + away_place(near)), (other, near)).start()

            return carry

        lax.fori_loop(0, FAR, early, 0)
        rows_arrive()
        for j in (0, ROWS - 1):
            tendency(j, tend, False)
        value = corner()
        for j in (0, ROWS - 1):
            at = pl.ds(3 * j * TILES + FULL, 1)
            tend[at, :] = jnp.where(lane[:1] < TAIL, tend[at, :], value[j : j + 1])
        for target in (2, 3, N_LON - 2, N_LON - 1):

            @pl.when(lon != target)
            def _():
                go(pair_of(target), (lat, target)).start()

        lax.fori_loop(FAR, N_LON, early, 0)

    @pl.when(polar)
    def _():
        at = pl.ds(pl.multiple_of(place(lon) * TILES, 8), BLOCK)
        gathered[at, :] = tend[pl.ds(pl.multiple_of(pair_of(lon) * TILES, 8), BLOCK), :]

    def complete(pair, lat_row):
        inverse = geo[lat_row * 4]
        first_at, last_at = pl.ds(0, N_LON, stride=TILES), pl.ds(FULL, N_LON, stride=TILES)
        first, last = gathered[first_at, :], gathered[last_at, :]
        spot = lax.broadcasted_iota(jnp.int32, (N_LON, LANES), 1)
        half = N_LON // 2
        after = jnp.concatenate([last[half:], pltpu.roll(last[:half], half - 1, 0)], axis=0)
        before = jnp.concatenate([pltpu.roll(last[half:], 1, 0), last[:half]], axis=0)

        def pick(value, part, to):
            return pltpu.roll(value, (LANES + to - TAIL - part * LEVELS) % LANES, 1)

        end = TAIL - LEVELS
        h_first, h_end, u_first, u_end = 0, 1, 2, 3
        field = pair % 3

        def put(east, west):
            gathered[last_at, :] = jnp.where(spot < end, last, jnp.where(spot < TAIL, last + east, 0.0))
            gathered[first_at, :] = jnp.where(spot < LEVELS, first + west, first)

        @pl.when(field == 0)
        def _():
            h, u = pick(last, h_end, end), pick(last, u_end, end)
            east = (u + pick(after, u_first, end)) * (h + pick(after, h_first, end)) - u * h
            h, u = pick(last, h_first, 0), pick(last, u_first, 0)
            west = (u + pick(before, u_end, 0)) * (h + pick(before, h_end, 0)) - u * h
            put(-0.25 * inverse * east, 0.25 * inverse * west)

        @pl.when(field == 1)
        def _():
            put(-0.5 * inverse * pick(after, h_first, end), 0.5 * inverse * pick(before, h_end, 0))

    def circle(pair, first_row):
        lat_row = first_row + pair // 3
        complete(pair, lat_row)
        cutoff = cut[lat_row]
        data = jnp.concatenate([gathered[pl.ds(0, SIDE), :], gathered[pl.ds(SIDE, SIDE), :]], axis=1)
        lines = dot(fore[...], data)
        real, imag = lines[:FREQ], lines[FREQ:]
        cosine, sine = twiddle[pl.ds(0, FREQ), :], twiddle[pl.ds(FREQ, FREQ), :]
        turned = jnp.concatenate([real * cosine + imag * sine, imag * cosine - real * sine], axis=1)
        spectrum = dot(turned, mix[...])
        wave = lax.broadcasted_iota(jnp.int32, (FREQ, 2 * LANES), 0) + BASE * (
            lax.broadcasted_iota(jnp.int32, (FREQ, 2 * LANES), 1) % LANES // LEVELS
        )
        wave = jnp.minimum(wave, NLON - wave)
        spectrum = jnp.where(wave <= cutoff, spectrum, 0.0)
        lines = dot(spectrum, unmix[...])
        real, imag = lines[:, : 2 * LANES], lines[:, 2 * LANES :]
        turned = jnp.concatenate([real * cosine - imag * sine, real * sine + imag * cosine], axis=0)
        result = dot(back[...], turned)
        sent_back[pl.ds(0, SIDE), :] = result[:, :LANES]
        sent_back[pl.ds(SIDE, SIDE), :] = result[:, LANES:]

    def home(pair, sector, device):
        return pltpu.make_async_remote_copy(
            block(sent_back, place(sector)), block(returned, pair), back_send, back_recv,
            device_id=device, device_id_type=MESH,
        )

    def own_block():
        return pltpu.make_async_copy(block(sent_back, place(lon)), block(returned, pair_of(lon)), keep_sem)

    def total(ref, blocks):
        return ref.at[pl.ds(0, blocks * BLOCK), :]

    def wait_for(ref, blocks, sem):
        pltpu.make_async_copy(total(ref, blocks), total(ref, blocks), sem).wait()

    @pl.when(lends)
    def _():
        for load in tables:
            load.wait()
        wait_for(gathered, N_LON, go_recv)
        circle(pair_of(OWN + away_place(lon)), other * ROWS)

        def away(i, carry):
            target = partner(i)
            home(pair_of(OWN + away_place(lon)), target, (other, target)).start()
            return carry

        lax.fori_loop(0, N_LON, away, 0)

    @pl.when(jnp.logical_not(polar))
    def _():
        rows_arrive()

    pltpu.make_async_copy(from_west, from_west, halo_recv.at[2]).wait()
    pltpu.make_async_copy(from_east, from_east, halo_recv.at[3]).wait()
    halos[0].wait_send()
    halos[1].wait_send()
    for i, f in enumerate(sides):
        at = pl.ds(SLOT + f * TILES + FULL, ROWS, stride=SLOT)
        here = from_east[pl.ds(i * ROWS, ROWS), :]
        cells[at, :] = jnp.where((lane >= TAIL) & (lane < TAIL + LEVELS), here, cells[at, :])
        at = pl.ds(SLOT + f * TILES + FULL + 1, ROWS, stride=SLOT)
        here = from_west[pl.ds(i * ROWS, ROWS), :]
        cells[at, :] = jnp.where(lane >= LANES - LEVELS, here, 0.0)

    @pl.when(jnp.logical_not(polar))
    def _():
        lax.fori_loop(0, ROWS, lambda j, c: (tendency(j, tend, True), c)[1], 0)
        pltpu.make_async_copy(tend, returned, keep_sem).start()

    def tracer(j, carry):
        inverse, sine, cos_north, cos_south = scalars(j)
        h, u, v, h_e, h_w, h_n, h_s, flux_e, flux_w, flux_n, flux_s = fluxes(j, cos_north, cos_south)
        for c in range(3):
            q, q_n, q_s = row(j + 1, 3 + c), row(j + 2, 3 + c), row(j, 3 + c)
            q_e, q_w = eastward(q), westward(q)
            zonal = flux_e * (0.5 * (q + q_e)) - flux_w * (0.5 * (q_w + q))
            merid = flux_n * (0.5 * (q + q_n)) - flux_s * (0.5 * (q_s + q))
            flux = (zonal + RATIO * merid) * inverse
            laplace = (q_e + q_w) + (q_n + q_s) - 4.0 * q
            at = pl.ds(pl.multiple_of((j * 3 + c) * TILES, 8), TILES)
            mass[at, :] = h * q + TIME_STEP * (DIFFUSION * laplace - flux)
        return carry

    lax.fori_loop(0, ROWS, tracer, 0)

    def narrow(j, carry):
        for t in range(FULL + 1):
            width = LANES if t < FULL else TAIL
            value = mass[pl.ds(j * 3 * TILES + t, 3, stride=TILES), :]
            mv[j, :, pl.ds(t * LANES, width)] = value[:, :width].astype(BF16)
        return carry

    lax.fori_loop(0, ROWS, narrow, 0)
    keep_mass = pltpu.make_async_copy(mv, mass_out, mass_sem)
    keep_mass.start()

    @pl.when(jnp.logical_not(lends))
    def _():
        for load in tables:
            load.wait()

    @pl.when(polar)
    def _():
        wait_for(gathered, N_LON - 1, go_recv)
        circle(pair_of(lon), lat * ROWS)

        def own(i, carry):
            target = partner(i)

            @pl.when(target != lon)
            def _():
                home(pair_of(lon), target, (lat, target)).start()

            return carry

        lax.fori_loop(0, N_LON, own, 0)
        own_block().start()

    halos[2].wait_send()
    halos[3].wait_send()
    keep_mass.wait()

    @pl.when(polar)
    def _():
        wait_for(tend, PAIRS - 1, go_send)
        wait_for(sent_back, N_LON - 1, back_send)
        own_block().wait()
        wait_for(tend, PAIRS - 1, back_recv)

    @pl.when(jnp.logical_not(polar))
    def _():
        pltpu.make_async_copy(tend, returned, keep_sem).wait()

    @pl.when(lends)
    def _():
        wait_for(sent_back, N_LON, back_send)


def finish(winds, thick, steps, mass, winds_out, thick_out, mass_out, wv, hv, sv, mv, in_sem, out_sem):
    def pair(n, source, held, target):
        return pltpu.make_async_copy(source, held, in_sem.at[n]), pltpu.make_async_copy(held, target, out_sem.at[n])

    mass_load, mass_store = pair(0, mass, mv, mass_out)
    wind_load, wind_store = pair(1, winds, wv, winds_out)
    thick_load, thick_store = pair(2, thick, hv, thick_out)
    steps_load = pltpu.make_async_copy(steps, sv, in_sem.at[3])
    for load in (steps_load, wind_load, thick_load, mass_load):
        load.start()
    steps_load.wait()
    wind_load.wait()

    def one_row(j, carry):
        for t in range(FULL + 1):
            width = LANES if t < FULL else TAIL
            at = pl.ds(t * LANES, width)
            step = sv[pl.ds((j * 3 + 1) * TILES + t, 2, stride=TILES), :]
            wv[j, :, at] = wv[j, :, at] + TIME_STEP * step[:, :width]
        return carry

    lax.fori_loop(0, ROWS, one_row, 0)
    wind_store.start()
    mass_load.wait()
    mass_store.start()
    thick_load.wait()
    for t in range(FULL + 1):
        width = LANES if t < FULL else TAIL
        at = pl.ds(t * LANES, width)
        hv[:, at] = hv[:, at] + TIME_STEP * sv[pl.ds(t, ROWS, stride=3 * TILES), :][:, :width]
    thick_store.start()
    for store in (wind_store, mass_store, thick_store):
        store.wait()


def local(winds, thickness, tracers, cutoff):
    fore, twiddle, mix, unmix, back = filter_tables()
    anywhere = pl.BlockSpec(memory_space=pl.ANY)
    side = pltpu.VMEM((48, LANES), F32)
    dma = pltpu.SemaphoreType.DMA
    rows = jax.ShapeDtypeStruct((PAIRS * TILES, LANES), F32)
    winds = jnp.transpose(winds, (1, 0, 2))
    tracers = jnp.transpose(tracers, (1, 0, 2))
    steps, mass = pl.pallas_call(
        kernel,
        out_shape=(rows, jax.ShapeDtypeStruct((ROWS, 3, WIDE), BF16)),
        in_specs=[anywhere] * 10,
        out_specs=(anywhere, anywhere),
        scratch_shapes=[
            pltpu.VMEM((ROWS, 2, WIDE), F32),
            pltpu.VMEM((ROWS, WIDE), F32),
            pltpu.VMEM((ROWS, 3, WIDE), BF16),
            pltpu.VMEM((ROWS, 3, WIDE), BF16),
            pltpu.VMEM((PAIRS * TILES, LANES), F32),
            pltpu.VMEM(((ROWS + 2) * SLOT, LANES), F32),
            side, side, side, side,
            pltpu.VMEM((PAIRS * TILES, LANES), F32),
            pltpu.VMEM((N_LON * TILES, LANES), F32),
            pltpu.VMEM((N_LON * TILES, LANES), F32),
            pltpu.VMEM(fore.shape, BF16),
            pltpu.VMEM(twiddle.shape, F32),
            pltpu.VMEM(mix.shape, BF16),
            pltpu.VMEM(unmix.shape, BF16),
            pltpu.VMEM(back.shape, BF16),
            pltpu.SMEM((NLAT,), jnp.int32),
            pltpu.SMEM((4 * NLAT,), F32),
            dma((5,)), dma((5,)), dma, dma, dma((4,)), dma((4,)), dma, dma, dma, dma,
        ],
        compiler_params=pltpu.CompilerParams(
            collective_id=0, has_side_effects=True, vmem_limit_bytes=VMEM_MIB * 1024 * 1024
        ),
        name="substep",
    )(cutoff, geometry(), winds, thickness, tracers, fore, twiddle, mix, unmix, back)
    new_winds, new_thickness, new_mass = pl.pallas_call(
        finish,
        out_shape=(
            jax.ShapeDtypeStruct((ROWS, 2, WIDE), F32),
            jax.ShapeDtypeStruct((ROWS, WIDE), F32),
            jax.ShapeDtypeStruct((ROWS, 3, WIDE), BF16),
        ),
        in_specs=[anywhere] * 4,
        out_specs=(anywhere,) * 3,
        scratch_shapes=[
            pltpu.VMEM((ROWS, 2, WIDE), F32),
            pltpu.VMEM((ROWS, WIDE), F32),
            pltpu.VMEM((PAIRS * TILES, LANES), F32),
            pltpu.VMEM((ROWS, 3, WIDE), BF16),
            dma((4,)), dma((3,)),
        ],
        compiler_params=pltpu.CompilerParams(vmem_limit_bytes=VMEM_MIB * 1024 * 1024),
        name="finish",
    )(winds, thickness, steps, mass)
    return jnp.transpose(new_winds, (1, 0, 2)), new_thickness, jnp.transpose(new_mass, (1, 0, 2))


def solution(mesh):
    in_specs = (P(None, "lat", "lon"), P("lat", "lon"), P(None, "lat", "lon"), P())
    out_specs = (P(None, "lat", "lon"), P("lat", "lon"), P(None, "lat", "lon"))
    return jax.shard_map(local, mesh=mesh, in_specs=in_specs, out_specs=out_specs, check_vma=False)
```
